32 devices in a mesh: batch: 4 (over y, x), seq: 2 (over core), fsdp: 4 (over z).
Axes of the slice: x: 2, y: 2, z: 4, core: 2. Of those that a mesh axis runs over, the one named last changes fastest.
Arguments:
- tokens: bfloat16 [16, 1024, 2048], P(('batch', 'fsdp'), 'seq'), may hold values from -6 to 6
- layer_inputs: bfloat16 [16, 1024, 256], P(('batch', 'fsdp'), 'seq'), may hold values from -6 to 6
- cotangent: bfloat16 [16, 1024, 2048], P(('batch', 'fsdp'), 'seq'), may hold values from -6 to 6
- doc_lengths: int32 [16, 4], P(('batch', 'fsdp')), may hold values from 1 to 1021, as said below
- w_query: bfloat16 [2048, 2048], P(('batch', 'seq', 'fsdp')), may hold values from -0.125 to 0.125
- w_key: bfloat16 [2048, 512], P(('batch', 'seq', 'fsdp')), may hold values from -0.125 to 0.125
- w_value: bfloat16 [2048, 512], P(('batch', 'seq', 'fsdp')), may hold values from -0.125 to 0.125
- w_output: bfloat16 [2048, 2048], P(('batch', 'seq', 'fsdp')), may hold values from -0.125 to 0.125
- laurel_left: bfloat16 [2048, 64], P(('batch', 'seq', 'fsdp')), may hold values from -0.125 to 0.125
- laurel_right: bfloat16 [2048, 64], P(('batch', 'seq', 'fsdp')), may hold values from -0.75 to 0.75
- w_gate: bfloat16 [2048, 8192], P(('batch', 'seq', 'fsdp')), may hold values from -0.125 to 0.125
- w_up: bfloat16 [2048, 8192], P(('batch', 'seq', 'fsdp')), may hold values from -0.125 to 0.125
- w_down: bfloat16 [2048, 8192], P(('batch', 'seq', 'fsdp')), may hold values from -0.0625 to 0.0625
- w_plgate: bfloat16 [2048, 256], P(('batch', 'seq', 'fsdp')), may hold values from -0.125 to 0.125
- w_plproj: bfloat16 [2048, 256], P(('batch', 'seq', 'fsdp')), may hold values from -0.375 to 0.375
- g_input: bfloat16 [2048], P(('batch', 'seq', 'fsdp')), may hold values from 0.25 to 1.75
- g_query: bfloat16 [256], P(('batch', 'seq', 'fsdp')), may hold values from 0.25 to 1.75
- g_key: bfloat16 [256], P(('batch', 'seq', 'fsdp')), may hold values from 0.25 to 1.75
- g_attn: bfloat16 [2048], P(('batch', 'seq', 'fsdp')), may hold values from 0.25 to 1.75
- g_laurel: bfloat16 [2048], P(('batch', 'seq', 'fsdp')), may hold values from 0.25 to 1.75
- g_preffw: bfloat16 [2048], P(('batch', 'seq', 'fsdp')), may hold values from 0.25 to 1.75
- g_ffw: bfloat16 [2048], P(('batch', 'seq', 'fsdp')), may hold values from 0.25 to 1.75
- g_perlayer: bfloat16 [2048], P(('batch', 'seq', 'fsdp')), may hold values from 0.25 to 1.75
Outputs:
- mixed: bfloat16 [16, 1024, 2048], P(('batch', 'fsdp'), 'seq')
- grad_tokens: float32 [16, 1024, 2048], P(('batch', 'fsdp'), 'seq')
- grad_query: float32 [2048, 2048], P(('batch', 'seq', 'fsdp'))
- grad_key: float32 [2048, 512], P(('batch', 'seq', 'fsdp'))
- grad_value: float32 [2048, 512], P(('batch', 'seq', 'fsdp'))
- grad_output: float32 [2048, 2048], P(('batch', 'seq', 'fsdp'))
- grad_left: float32 [2048, 64], P(('batch', 'seq', 'fsdp'))
- grad_right: float32 [2048, 64], P(('batch', 'seq', 'fsdp'))
- grad_gate: float32 [2048, 8192], P(('batch', 'seq', 'fsdp'))
- grad_up: float32 [2048, 8192], P(('batch', 'seq', 'fsdp'))
- grad_down: float32 [2048, 8192], P(('batch', 'seq', 'fsdp'))
- grad_plgate: float32 [2048, 256], P(('batch', 'seq', 'fsdp'))
- grad_plproj: float32 [2048, 256], P(('batch', 'seq', 'fsdp'))
- grad_g_input: float32 [2048], P(('batch', 'seq', 'fsdp'))
- grad_g_query: float32 [256], P(('batch', 'seq', 'fsdp'))
- grad_g_key: float32 [256], P(('batch', 'seq', 'fsdp'))
- grad_g_attn: float32 [2048], P(('batch', 'seq', 'fsdp'))
- grad_g_laurel: float32 [2048], P(('batch', 'seq', 'fsdp'))
- grad_g_preffw: float32 [2048], P(('batch', 'seq', 'fsdp'))
- grad_g_ffw: float32 [2048], P(('batch', 'seq', 'fsdp'))
- grad_g_perlayer: float32 [2048], P(('batch', 'seq', 'fsdp'))
The draws below stay inside these ranges and needn't reach their ends.
Inputs may be any that keep to these rules, and one draw needn't show every extreme that they name: `doc_lengths`: each row holds the lengths of 4 documents packed in order into one sequence; they sum to 1024. The first is under 512, the last two are under 512 // 2. In one row, drawn from the seed, the first and the last two are 1 and the second is 1021.
All inputs are finite; a program needn't handle non-finite values.
Results may differ from the reference program's by a relative error of at most 0.02.
Values may be sent and summed in bfloat16 or wider, within the bound.
A program may use at most 704 MiB of HBM per device.

```python
import jax
import jax.numpy as jnp
from jax import lax

D = 2048
HEADS = 8
KV = 2
HD = 256
FF = 8192
RANK = 64
PLD = 256
WINDOW = 512
SEQ_LEN = 1024
TOK_SEQ = 512
SEQS = 16


def draw_doc_lengths(key, part):
    key = jax.random.fold_in(key, 7)
    key_head, key_tail, key_pick = jax.random.split(key, 3)
    head_len = jax.random.randint(key_head, (SEQS,), 1, TOK_SEQ)
    tail_lens = jax.random.randint(key_tail, (SEQS, 2), 1, TOK_SEQ // 2)
    picked = jax.random.randint(key_pick, (), 0, SEQS)
    chosen_row = jnp.arange(SEQS, dtype=jnp.int32) == picked
    head_len = jnp.where(chosen_row, 1, head_len)
    tail_lens = jnp.where(chosen_row[:, None], 1, tail_lens)
    middle = SEQ_LEN - head_len - tail_lens[:, 0] - tail_lens[:, 1]
    return jnp.stack([head_len, middle, tail_lens[:, 0], tail_lens[:, 1]], 1).astype(jnp.int32)


def level_of(own_key, extent, shards, least, top_value):
    factor_of = 1.0
    for position, blocks in shards:
        heights = jax.random.uniform(jax.random.fold_in(jax.random.fold_in(own_key, 6), position), (blocks,), jnp.float32, least / len(shards), top_value / len(shards))
        factor_of = factor_of * jnp.repeat(jnp.exp(heights), extent[position] // blocks).reshape((-1,) + (1,) * (len(extent) - 1 - position))
    return factor_of


def noise(own_key, extent, spread, limit, shards=(), held_as=jnp.bfloat16):
    values = jax.random.normal(own_key, extent, jnp.float32) * spread
    if len(shards) > 0:
        values = level_of(own_key, extent, shards, -0.22, 0.18) * values
    return jnp.clip(values, min=-limit, max=limit).astype(held_as)


def setup_inputs(seed: int = 0) -> dict:
    key_of = jax.random.split(jax.random.key(seed), 24)
    return {
        "tokens": noise(key_of[0], (SEQS, SEQ_LEN, D), 1.0, 6.0, ((0, 16), (1, 2))),
        "layer_inputs": noise(key_of[1], (SEQS, SEQ_LEN, PLD), 1.0, 6.0, ((0, 16), (1, 2))),
        "cotangent": noise(key_of[2], (SEQS, SEQ_LEN, D), 1.0, 6.0, ((0, 16), (1, 2))),
        "doc_lengths": draw_doc_lengths(jax.random.fold_in(key_of[23], 71), 0),
        "w_query": noise(key_of[4], (D, HEADS * HD), D ** -0.5, 0.125, ((0, 32),)),
        "w_key": noise(key_of[5], (D, KV * HD), D ** -0.5, 0.125, ((0, 32),)),
        "w_value": noise(key_of[6], (D, KV * HD), D ** -0.5, 0.125, ((0, 32),)),
        "w_output": noise(key_of[7], (D, HEADS * HD), (HEADS * HD) ** -0.5, 0.125, ((0, 32),)),
        "laurel_left": noise(key_of[8], (D, RANK), D ** -0.5, 0.125, ((0, 32),)),
        "laurel_right": noise(key_of[9], (D, RANK), RANK ** -0.5, 0.75, ((0, 32),)),
        "w_gate": noise(key_of[10], (D, FF), D ** -0.5, 0.125, ((0, 32),)),
        "w_up": noise(key_of[11], (D, FF), D ** -0.5, 0.125, ((0, 32),)),
        "w_down": noise(key_of[12], (D, FF), FF ** -0.5, 0.0625, ((0, 32),)),
        "w_plgate": noise(key_of[13], (D, PLD), D ** -0.5, 0.125, ((0, 32),)),
        "w_plproj": noise(key_of[14], (D, PLD), PLD ** -0.5, 0.375, ((0, 32),)),
        "g_input": jnp.clip(1.0 + 0.15 * jax.random.normal(key_of[15], (D,), jnp.float32), 0.25, 1.75).astype(jnp.bfloat16),
        "g_query": jnp.clip(1.0 + 0.15 * jax.random.normal(key_of[16], (HD,), jnp.float32), 0.25, 1.75).astype(jnp.bfloat16),
        "g_key": jnp.clip(1.0 + 0.15 * jax.random.normal(key_of[17], (HD,), jnp.float32), 0.25, 1.75).astype(jnp.bfloat16),
        "g_attn": jnp.clip(1.0 + 0.15 * jax.random.normal(key_of[18], (D,), jnp.float32), 0.25, 1.75).astype(jnp.bfloat16),
        "g_laurel": jnp.clip(1.0 + 0.15 * jax.random.normal(key_of[19], (D,), jnp.float32), 0.25, 1.75).astype(jnp.bfloat16),
        "g_preffw": jnp.clip(1.0 + 0.15 * jax.random.normal(key_of[20], (D,), jnp.float32), 0.25, 1.75).astype(jnp.bfloat16),
        "g_ffw": jnp.clip(1.0 + 0.15 * jax.random.normal(key_of[21], (D,), jnp.float32), 0.25, 1.75).astype(jnp.bfloat16),
        "g_perlayer": jnp.clip(1.0 + 0.15 * jax.random.normal(key_of[22], (D,), jnp.float32), 0.25, 1.75).astype(jnp.bfloat16),
    }


EPS = 1e-06
THETA = 10000.0
ROOT_HALF = 0.7071067811865476

@jax.custom_vjp
def low(v):
    return lax.optimization_barrier(v.astype(jnp.bfloat16)).astype(jnp.float32)

@jax.custom_vjp
def low_back(v):
    return v

def low_keep(v):
    return (low(v), None)

def low_pass(kept, grad):
    return (grad,)

def back_keep(v):
    return (v, None)

def back_low(kept, grad):
    return (low(grad),)
low.defvjp(low_keep, low_pass)
low_back.defvjp(back_keep, back_low)

def rms_norm(values, weight):
    return values * lax.rsqrt(lax.optimization_barrier(jnp.mean(values * values, -1, keepdims=True)) + EPS) * weight

def geglu(gate_in, factor):
    return jax.nn.gelu(gate_in, approximate=True) * factor

def positions_of(places, lengths):
    doc_ends = jnp.cumsum(lengths).astype(jnp.int32)
    starts = (doc_ends - lengths).astype(jnp.int32)
    segment = lax.optimization_barrier(jnp.sum((places[:, None] >= doc_ends[None, :]).astype(jnp.int32), 1)).astype(jnp.int32)
    chosen = segment[:, None] == jnp.arange(lengths.shape[0], dtype=jnp.int32)[None, :]
    offset = lax.optimization_barrier(jnp.sum(jnp.where(chosen, starts[None, :], 0), 1)).astype(jnp.int32)
    return (segment, (places - offset).astype(jnp.float32))

def rope_tables(rel_pos, width_all):
    half_width = width_all // 2
    frequency = THETA ** (-jnp.arange(half_width, dtype=jnp.float32) * 2.0 / width_all)
    angles = rel_pos[:, None] * frequency[None, :]
    return (jnp.cos(angles)[:, None, :], jnp.sin(angles)[:, None, :])

def rotate(values, cosine_table, sine_table):
    half_width = values.shape[-1] // 2
    leading = values[..., :half_width]
    trailing = values[..., half_width:]
    return jnp.concatenate([leading * cosine_table - trailing * sine_table, trailing * cosine_table + leading * sine_table], -1)

def matmul(left, right):
    return jnp.dot(left, right, precision=lax.Precision.HIGHEST)

def one_sequence(params, tokens_row, perlayer_row, lengths):
    query_w, key_w, value_w, output_w, left_w, right_w, gate_w, up_w, down_w, plgate_w, plproj_w, input_g, query_g, key_g, attn_g, laurel_g, preffw_g, ffw_g, perlayer_g = params
    tok_rows = tokens_row.shape[0]
    head_dim = query_g.shape[0]
    num_heads = query_w.shape[1] // head_dim
    kv_heads = key_w.shape[1] // head_dim
    groups = num_heads // kv_heads
    places = jnp.arange(tok_rows, dtype=jnp.int32)
    segment, rel_pos = positions_of(places, lengths)
    cosine_table, sine_table = rope_tables(rel_pos, head_dim)
    x_normed = rms_norm(tokens_row, input_g)
    x_low = low(x_normed)
    query_raw = low_back(matmul(x_low, query_w)).reshape(tok_rows, num_heads, head_dim)
    key_raw = low_back(matmul(x_low, key_w)).reshape(tok_rows, kv_heads, head_dim)
    value_low = low(low_back(matmul(x_low, value_w))).reshape(tok_rows, kv_heads, head_dim)
    query_low = low(rotate(rms_norm(query_raw, query_g), cosine_table, sine_table))
    query_group = query_low.reshape(tok_rows, kv_heads, groups, head_dim)
    key_low = low(rotate(rms_norm(key_raw, key_g), cosine_table, sine_table))
    distance = places[:, None] - places[None, :]
    allowed = (segment[:, None] == segment[None, :]) & (distance >= 0) & (distance < WINDOW)
    scores = low_back(jnp.einsum('tkgd,skd->kgts', query_group, key_low, precision=lax.Precision.HIGHEST) * head_dim ** (-0.5))
    attn_probs = jax.nn.softmax(jnp.where(allowed, scores, -1e+30), axis=-1)
    attn_heads = jnp.einsum('kgts,skd->tkgd', low(attn_probs), value_low, precision=lax.Precision.HIGHEST)
    attn_low = low(low_back(attn_heads.reshape(tok_rows, num_heads * head_dim)))
    attn_proj = low_back(matmul(attn_low, output_w.T))
    left_low = low(low_back(matmul(x_low, left_w)))
    right_out = low_back(matmul(left_low, right_w.T))
    hidden = (tokens_row + rms_norm(attn_proj, attn_g) + x_normed + rms_norm(right_out, laurel_g)) * ROOT_HALF
    ffw_in = low(rms_norm(hidden, preffw_g))
    gate_out = low_back(matmul(ffw_in, gate_w))
    up_out = low_back(matmul(ffw_in, up_w))
    act_low = low(geglu(gate_out, up_out))
    down_out = low_back(matmul(act_low, down_w.T))
    second = hidden + rms_norm(down_out, ffw_g)
    second_low = low(second)
    plgate_out = low_back(matmul(second_low, plgate_w))
    gated_low = low(geglu(plgate_out, perlayer_row))
    plproj_out = low_back(matmul(gated_low, plproj_w.T))
    return second + rms_norm(plproj_out, perlayer_g)

def reference(tokens, layer_inputs, cotangent, doc_lengths, w_query, w_key, w_value, w_output, laurel_left, laurel_right, w_gate, w_up, w_down, w_plgate, w_plproj, g_input, g_query, g_key, g_attn, g_laurel, g_preffw, g_ffw, g_perlayer):
    params = tuple((entry.astype(jnp.float32) for entry in (w_query, w_key, w_value, w_output, laurel_left, laurel_right, w_gate, w_up, w_down, w_plgate, w_plproj, g_input, g_query, g_key, g_attn, g_laurel, g_preffw, g_ffw, g_perlayer)))
    inputs = tokens.astype(jnp.float32)
    perlayer = layer_inputs.astype(jnp.float32)

    def layer(weights, values):

        def scan_step(unused, sequence_item):
            return (unused, jax.checkpoint(one_sequence)(weights, sequence_item[0], sequence_item[1], sequence_item[2]))
        unused, stacked = lax.scan(scan_step, jnp.zeros((), jnp.float32), (values, perlayer, doc_lengths))
        return stacked
    outputs, pull = jax.vjp(layer, params, inputs)
    grad_params, grad_inputs = pull(cotangent.astype(jnp.float32))
    grad_query, grad_key, grad_value, grad_output, grad_left, grad_right, grad_gate, grad_up, grad_down, grad_plgate, grad_plproj, grad_g_input, grad_g_query, grad_g_key, grad_g_attn, grad_g_laurel, grad_g_preffw, grad_g_ffw, grad_g_perlayer = grad_params
    return (outputs.astype(jnp.bfloat16), grad_inputs, grad_query, grad_key, grad_value, grad_output, grad_left, grad_right, grad_gate, grad_up, grad_down, grad_plgate, grad_plproj, grad_g_input, grad_g_query, grad_g_key, grad_g_attn, grad_g_laurel, grad_g_preffw, grad_g_ffw, grad_g_perlayer)
```

```python
import jax
import jax.numpy as jnp
from jax import lax
from jax.sharding import PartitionSpec as P

WINDOW = 512
ALL_AXES = ("batch", "seq", "fsdp")
ROW_AXES = ("batch", "fsdp")


EPS = 1e-06
THETA = 10000.0
ROOT_HALF = 0.7071067811865476


def shifted(array, axis, by):
    count = lax.axis_size(axis)
    pairs = [(i, i + by) for i in range(count) if 0 <= i + by < count]
    return lax.ppermute(array, axis, pairs)


def rms_norm(values, weight):
    return values * lax.rsqrt(jnp.mean(values * values, -1, keepdims=True) + EPS) * weight


def norm_back(values, weight, upstream):
    normed, pull = jax.vjp(rms_norm, values, weight)
    return pull(upstream)


def geglu(gate_in, factor):
    return jax.nn.gelu(gate_in, approximate=True) * factor


def positions_of(places, lengths):
    doc_ends = jnp.cumsum(lengths)
    starts = doc_ends - lengths
    segment = jnp.sum((places[:, None] >= doc_ends[None, :]).astype(jnp.int32), 1)
    chosen = segment[:, None] == jnp.arange(lengths.shape[0], dtype=jnp.int32)[None, :]
    offset = jnp.sum(jnp.where(chosen, starts[None, :], 0), 1)
    return (segment, (places - offset).astype(jnp.float32))


def rope_tables(rel_pos, width_all):
    half_width = width_all // 2
    frequency = THETA ** (-jnp.arange(half_width, dtype=jnp.float32) * 2.0 / width_all)
    angles = rel_pos[:, None] * frequency[None, :]
    return (jnp.cos(angles)[:, None, :], jnp.sin(angles)[:, None, :])


def rotate(values, cosine_table, sine_table):
    half_width = values.shape[-1] // 2
    leading = values[..., :half_width]
    trailing = values[..., half_width:]
    return jnp.concatenate(
        [
            leading * cosine_table - trailing * sine_table,
            trailing * cosine_table + leading * sine_table,
        ],
        -1,
    )


def rotate_back(upstream, cosine_table, sine_table):
    half_width = upstream.shape[-1] // 2
    leading = upstream[..., :half_width]
    trailing = upstream[..., half_width:]
    return jnp.concatenate(
        [
            leading * cosine_table + trailing * sine_table,
            trailing * cosine_table - leading * sine_table,
        ],
        -1,
    )


def project(left, right):
    return jnp.dot(left, right, preferred_element_type=jnp.float32)


def against_rows(left, right):
    return lax.dot_general(
        left, right, (((1,), (1,)), ((), ())), preferred_element_type=jnp.float32
    )


def over_tokens(left, right):
    return lax.dot_general(
        left, right, (((0,), (0,)), ((), ())), preferred_element_type=jnp.float32
    )


def split_columns(packed, widths):
    pieces = []
    column_at = 0
    for width_one in widths:
        pieces.append(packed[:, column_at : column_at + width_one])
        column_at = column_at + width_one
    return pieces


def whole_gather_plan(
    tokens,
    layer_inputs,
    cotangent,
    doc_lengths,
    w_query,
    w_key,
    w_value,
    w_output,
    laurel_left,
    laurel_right,
    w_gate,
    w_up,
    w_down,
    w_plgate,
    w_plproj,
    g_input,
    g_query,
    g_key,
    g_attn,
    g_laurel,
    g_preffw,
    g_ffw,
    g_perlayer,
):
    gathered = (
        lax.all_gather(w_query, ALL_AXES, axis=0, tiled=True),
        lax.all_gather(w_key, ALL_AXES, axis=0, tiled=True),
        lax.all_gather(w_value, ALL_AXES, axis=0, tiled=True),
        lax.all_gather(w_output, ALL_AXES, axis=0, tiled=True),
        lax.all_gather(laurel_left, ALL_AXES, axis=0, tiled=True),
        lax.all_gather(laurel_right, ALL_AXES, axis=0, tiled=True),
        lax.all_gather(w_gate, ALL_AXES, axis=0, tiled=True),
        lax.all_gather(w_up, ALL_AXES, axis=0, tiled=True),
        lax.all_gather(w_down, ALL_AXES, axis=0, tiled=True),
        lax.all_gather(w_plgate, ALL_AXES, axis=0, tiled=True),
        lax.all_gather(w_plproj, ALL_AXES, axis=0, tiled=True),
        lax.all_gather(g_input, ALL_AXES, axis=0, tiled=True),
        lax.all_gather(g_query, ALL_AXES, axis=0, tiled=True),
        lax.all_gather(g_key, ALL_AXES, axis=0, tiled=True),
        lax.all_gather(g_attn, ALL_AXES, axis=0, tiled=True),
        lax.all_gather(g_laurel, ALL_AXES, axis=0, tiled=True),
        lax.all_gather(g_preffw, ALL_AXES, axis=0, tiled=True),
        lax.all_gather(g_ffw, ALL_AXES, axis=0, tiled=True),
        lax.all_gather(g_perlayer, ALL_AXES, axis=0, tiled=True),
    )
    query_w, key_w, value_w, output_w, left_w, right_w, gate_w, up_w, down_w, plgate_w, plproj_w = (
        gathered[:11]
    )
    input_g, query_g, key_g, attn_g, laurel_g, preffw_g, ffw_g, perlayer_g = [
        entry.astype(jnp.float32) for entry in gathered[11:]
    ]
    head_dim = query_g.shape[0]
    num_heads = query_w.shape[1] // head_dim
    kv_heads = key_w.shape[1] // head_dim
    groups = num_heads // kv_heads
    width_kv = kv_heads * head_dim
    score_scale = head_dim ** (-0.5)
    seq_pos = lax.axis_index("seq")
    tok_rows = tokens.shape[1]
    reach_hops = min((WINDOW - 2) // tok_rows + 1, lax.axis_size("seq") - 1)
    resid_in = tokens[0].astype(jnp.float32)
    perlayer = layer_inputs[0].astype(jnp.float32)
    upstream = cotangent[0].astype(jnp.float32)
    lengths = doc_lengths[0]
    places = seq_pos * tok_rows + jnp.arange(tok_rows, dtype=jnp.int32)
    segment, rel_pos = positions_of(places, lengths)
    cosine_table, sine_table = rope_tables(rel_pos, head_dim)
    ff_width = gate_w.shape[1]
    x_normed = rms_norm(resid_in, input_g)
    x_low = x_normed.astype(jnp.bfloat16)
    query_heads = project(x_low, query_w).reshape(tok_rows, num_heads, head_dim)
    key_heads = project(x_low, key_w).reshape(tok_rows, kv_heads, head_dim)
    value_raw = project(x_low, value_w)
    query_low = rotate(rms_norm(query_heads, query_g), cosine_table, sine_table).astype(
        jnp.bfloat16
    )
    key_rot = rotate(rms_norm(key_heads, key_g), cosine_table, sine_table)
    kv_local = jnp.concatenate([key_rot.reshape(tok_rows, width_kv), value_raw], 1).astype(
        jnp.bfloat16
    )
    pieces = []
    for distance in range(reach_hops, 0, -1):
        pieces.append(shifted(kv_local, "seq", distance))
    kv_window = jnp.concatenate(pieces + [kv_local], 0)
    key_places = (seq_pos - reach_hops) * tok_rows + jnp.arange(
        (reach_hops + 1) * tok_rows, dtype=jnp.int32
    )
    key_segment, key_rel = positions_of(key_places, lengths)
    distance_all = places[:, None] - key_places[None, :]
    allowed = (
        (segment[:, None] == key_segment[None, :])
        & (distance_all >= 0)
        & (distance_all < WINDOW)
        & (key_places[None, :] >= 0)
    )
    keys_win = kv_window[:, :width_kv].reshape(-1, kv_heads, head_dim)
    values_win = kv_window[:, width_kv:].reshape(-1, kv_heads, head_dim)
    query_group = query_low.reshape(tok_rows, kv_heads, groups, head_dim)

    def scores_of():
        raw_scores = (
            jnp.einsum("tkgd,skd->kgts", query_group, keys_win, preferred_element_type=jnp.float32)
            * score_scale
        )
        return jnp.where(allowed, raw_scores, -1e30)

    scores = scores_of()
    row_max = jnp.max(scores, -1, keepdims=True)
    row_total = jnp.sum(jnp.exp(scores - row_max), -1, keepdims=True)
    log_total = row_max + jnp.log(row_total)
    attn_probs = jnp.exp(scores - log_total)
    attn_heads = jnp.einsum(
        "kgts,skd->tkgd",
        attn_probs.astype(jnp.bfloat16),
        values_win,
        preferred_element_type=jnp.float32,
    )
    attn_low = attn_heads.reshape(tok_rows, num_heads * head_dim).astype(jnp.bfloat16)
    attn_proj = against_rows(attn_low, output_w)
    left_low = project(x_low, left_w).astype(jnp.bfloat16)
    right_out = against_rows(left_low, right_w)
    hidden = (
        resid_in + rms_norm(attn_proj, attn_g) + x_normed + rms_norm(right_out, laurel_g)
    ) * ROOT_HALF
    ffw_in = rms_norm(hidden, preffw_g).astype(jnp.bfloat16)
    gate_used, up_used, down_used = (gate_w, up_w, down_w)
    gate_out = project(ffw_in, gate_used)
    up_out = project(ffw_in, up_used)
    act_low = geglu(gate_out, up_out).astype(jnp.bfloat16)
    down_terms = against_rows(act_low, down_used)
    second = hidden + rms_norm(down_terms, ffw_g)
    second_low = second.astype(jnp.bfloat16)
    plgate_out = project(second_low, plgate_w)
    gated_low = geglu(plgate_out, perlayer).astype(jnp.bfloat16)
    plproj_out = against_rows(gated_low, plproj_w)
    mixed_out = (second + rms_norm(plproj_out, perlayer_g)).astype(jnp.bfloat16)
    d_plproj, d_perlayer_g = norm_back(plproj_out, perlayer_g, upstream)
    d_plproj_low = d_plproj.astype(jnp.bfloat16)
    d_gated = project(d_plproj_low, plproj_w)
    d_plgate_low = jax.vjp(geglu, plgate_out, perlayer)[1](d_gated)[0].astype(jnp.bfloat16)
    d_second = upstream + against_rows(d_plgate_low, plgate_w)
    d_down, d_ffw_g = norm_back(down_terms, ffw_g, d_second)
    d_down_low = d_down.astype(jnp.bfloat16)
    d_act = project(d_down_low, down_used)
    d_gate, d_up = jax.vjp(geglu, gate_out, up_out)[1](d_act)
    d_gate_low = d_gate.astype(jnp.bfloat16)
    d_up_low = d_up.astype(jnp.bfloat16)
    d_ffw_terms = against_rows(d_gate_low, gate_used) + against_rows(d_up_low, up_used)
    d_hidden_norm, d_preffw_g = norm_back(hidden, preffw_g, d_ffw_terms)
    d_branch = (d_second + d_hidden_norm) * ROOT_HALF
    ffn_grads = lax.psum_scatter(
        jnp.concatenate(
            [
                over_tokens(ffw_in, d_gate_low),
                over_tokens(ffw_in, d_up_low),
                over_tokens(d_down_low, act_low),
            ],
            1,
        ),
        ALL_AXES,
        scatter_dimension=0,
        tiled=True,
    )
    d_laurel, d_laurel_g = norm_back(right_out, laurel_g, d_branch)
    d_laurel_low = d_laurel.astype(jnp.bfloat16)
    d_left_low = project(d_laurel_low, right_w).astype(jnp.bfloat16)
    d_attn, d_attn_g = norm_back(attn_proj, attn_g, d_branch)
    d_attn_low = d_attn.astype(jnp.bfloat16)
    d_heads = project(d_attn_low, output_w).astype(jnp.bfloat16)
    d_group = d_heads.reshape(tok_rows, kv_heads, groups, head_dim)
    scores = scores_of()
    attn_probs = jnp.exp(scores - log_total)
    d_probs = jnp.einsum("tkgd,skd->kgts", d_group, values_win, preferred_element_type=jnp.float32)
    d_scores = (attn_probs * (d_probs - jnp.sum(attn_probs * d_probs, -1, keepdims=True))).astype(
        jnp.bfloat16
    )
    d_query_rot = (
        jnp.einsum("kgts,skd->tkgd", d_scores, keys_win, preferred_element_type=jnp.float32)
        * score_scale
    )
    d_keys = (
        jnp.einsum("kgts,tkgd->skd", d_scores, query_group, preferred_element_type=jnp.float32)
        * score_scale
    )
    d_values = jnp.einsum(
        "kgts,tkgd->skd",
        attn_probs.astype(jnp.bfloat16),
        d_group,
        preferred_element_type=jnp.float32,
    )
    d_kv = jnp.concatenate([d_keys.reshape(-1, width_kv), d_values.reshape(-1, width_kv)], 1)
    d_kv_local = d_kv[reach_hops * tok_rows :]
    for distance in range(reach_hops, 0, -1):
        piece_grad = d_kv[
            (reach_hops - distance) * tok_rows : (reach_hops - distance + 1) * tok_rows
        ]
        d_kv_local = d_kv_local + shifted(piece_grad.astype(jnp.bfloat16), "seq", -distance).astype(
            piece_grad.dtype
        )
    d_key_rot = d_kv_local[:, :width_kv].reshape(tok_rows, kv_heads, head_dim)
    d_value_low = d_kv_local[:, width_kv:].astype(jnp.bfloat16)
    d_query_norm = rotate_back(
        d_query_rot.reshape(tok_rows, num_heads, head_dim), cosine_table, sine_table
    )
    d_query_raw, d_query_g = norm_back(query_heads, query_g, d_query_norm)
    d_key_norm = rotate_back(d_key_rot, cosine_table, sine_table)
    d_key_raw, d_key_g = norm_back(key_heads, key_g, d_key_norm)
    d_query_low = d_query_raw.reshape(tok_rows, num_heads * head_dim).astype(jnp.bfloat16)
    d_key_low = d_key_raw.reshape(tok_rows, width_kv).astype(jnp.bfloat16)
    d_x_low = (
        against_rows(d_query_low, query_w)
        + against_rows(d_key_low, key_w)
        + against_rows(d_value_low, value_w)
        + against_rows(d_left_low, left_w)
    )
    d_input, d_input_g = norm_back(resid_in, input_g, d_x_low + d_branch)
    grad_tokens = (d_input + d_branch)[None]
    other_grads = lax.psum_scatter(
        jnp.concatenate(
            [
                over_tokens(x_low, d_query_low),
                over_tokens(x_low, d_key_low),
                over_tokens(x_low, d_value_low),
                over_tokens(d_attn_low, attn_low),
                over_tokens(x_low, d_left_low),
                over_tokens(d_laurel_low, left_low),
                over_tokens(second_low, d_plgate_low),
                over_tokens(d_plproj_low, gated_low),
            ],
            1,
        ),
        ALL_AXES,
        scatter_dimension=0,
        tiled=True,
    )
    other_widths = [
        query_w.shape[1],
        key_w.shape[1],
        value_w.shape[1],
        output_w.shape[1],
        left_w.shape[1],
        right_w.shape[1],
        plgate_w.shape[1],
        plproj_w.shape[1],
    ]
    (
        grad_query,
        grad_key,
        grad_value,
        grad_output,
        grad_left,
        grad_right,
        grad_plgate,
        grad_plproj,
    ) = split_columns(other_grads, other_widths)
    grad_gate, grad_up, grad_down = split_columns(ffn_grads, [ff_width, ff_width, ff_width])
    (
        grad_g_input,
        grad_g_query,
        grad_g_key,
        grad_g_attn,
        grad_g_laurel,
        grad_g_preffw,
        grad_g_ffw,
        grad_g_perlayer,
    ) = (
        lax.psum_scatter(d_input_g, ALL_AXES, scatter_dimension=0, tiled=True),
        lax.psum_scatter(d_query_g, ALL_AXES, scatter_dimension=0, tiled=True),
        lax.psum_scatter(d_key_g, ALL_AXES, scatter_dimension=0, tiled=True),
        lax.psum_scatter(d_attn_g, ALL_AXES, scatter_dimension=0, tiled=True),
        lax.psum_scatter(d_laurel_g, ALL_AXES, scatter_dimension=0, tiled=True),
        lax.psum_scatter(d_preffw_g, ALL_AXES, scatter_dimension=0, tiled=True),
        lax.psum_scatter(d_ffw_g, ALL_AXES, scatter_dimension=0, tiled=True),
        lax.psum_scatter(d_perlayer_g, ALL_AXES, scatter_dimension=0, tiled=True),
    )
    return (
        mixed_out[None],
        grad_tokens,
        grad_query,
        grad_key,
        grad_value,
        grad_output,
        grad_left,
        grad_right,
        grad_gate,
        grad_up,
        grad_down,
        grad_plgate,
        grad_plproj,
        grad_g_input,
        grad_g_query,
        grad_g_key,
        grad_g_attn,
        grad_g_laurel,
        grad_g_preffw,
        grad_g_ffw,
        grad_g_perlayer,
    )


BF16 = jnp.bfloat16
X_PAIRS = [(0, 1), (1, 0), (2, 3), (3, 2)]
Y_PAIRS = [(0, 2), (2, 0), (1, 3), (3, 1)]
CORE_PAIRS = [(0, 1), (1, 0)]


def swap_x(array):
    return lax.ppermute(array, "batch", X_PAIRS)


def swap_y(array):
    return lax.ppermute(array, "batch", Y_PAIRS)


def swap_core(array):
    return lax.ppermute(array, "seq", CORE_PAIRS)


def chained(swap, pieces, earlier=()):
    there = list(earlier)
    for piece in pieces:
        there.append(swap(after(piece, there[-2]) if len(there) > 1 else piece))
    return there[len(earlier) :]


def pick(array, axis, index):
    return lax.dynamic_index_in_dim(array, index, axis, keepdims=False)


def in_order(index, mine, theirs, axis):
    first = jnp.where(index == 0, mine, theirs)
    second = jnp.where(index == 0, theirs, mine)
    return jnp.stack([first, second], axis)


def halves_by(index, array, axis):
    low, high = jnp.split(array, 2, axis)
    return jnp.concatenate(
        [jnp.where(index == 0, low, high), jnp.where(index == 0, high, low)], axis
    )


def to_pairs(x_at, array, axis):
    b0, b1, b2, b3 = jnp.split(array, 4, axis)
    even = x_at == 0
    return jnp.concatenate(
        [
            jnp.where(even, b0, b1),
            jnp.where(even, b2, b3),
            jnp.where(even, b1, b0),
            jnp.where(even, b3, b2),
        ],
        axis,
    )


def from_pairs(x_at, array, axis):
    e0, e1, e2, e3 = jnp.split(array, 4, axis)
    even = x_at == 0
    return jnp.concatenate(
        [
            jnp.where(even, e0, e2),
            jnp.where(even, e2, e0),
            jnp.where(even, e1, e3),
            jnp.where(even, e3, e1),
        ],
        axis,
    )


def after(array, earlier):
    return lax.optimization_barrier((array, earlier))[0]


def gather_z(array):
    kinds, rows, width = array.shape
    stacked = lax.all_gather(array, "fsdp", axis=0, tiled=False)
    return [stacked[:, kind].reshape(-1, width) for kind in range(kinds)]


def scatter_z(ordered):
    count, kinds, rows, width = ordered.shape
    flat = ordered.reshape(count * kinds * rows, width)
    return lax.psum_scatter(flat, "fsdp", scatter_dimension=0, tiled=True)


def scatter_z_small(ordered):
    count = lax.axis_size("fsdp")
    z_at = lax.axis_index("fsdp")
    total = pick(ordered, 0, z_at).astype(jnp.float32)
    for by in range(1, count):
        turn = [(i, (i + by) % count) for i in range(count)]
        sent = pick(ordered, 0, lax.rem(z_at + by, count))
        total = total + lax.ppermute(sent, "fsdp", turn).astype(jnp.float32)
    return total.astype(BF16)


def sum_all(array):
    array = array + swap_core(array)
    array = array + swap_x(array)
    array = array + swap_y(array)
    count = lax.axis_size("fsdp")
    turns = [
        lax.ppermute(array, "fsdp", [(i, (i + by) % count) for i in range(count)])
        for by in range(1, count)
    ]
    return sum(turns, array)


def gate_up_act(left, gate_w, up_w):
    gate, up = project(left, gate_w), project(left, up_w)
    return gate.astype(BF16), up.astype(BF16), geglu(gate, up).astype(BF16)


def gate_up_back(left, down_w, gate, up):
    gate, up = gate.astype(jnp.float32), up.astype(jnp.float32)
    d_gate, d_up = jax.vjp(geglu, gate, up)[1](project(left, down_w))
    return d_gate.astype(BF16), d_up.astype(BF16)


def onto_model(lefts, weights):
    half = lefts[0].shape[0] // 2

    def total(cut):
        terms = [against_rows(left[cut], weight) for left, weight in zip(lefts, weights)]
        return sum(terms[1:], terms[0])

    return total(slice(0, half)), total(slice(half, None)).astype(BF16)


def weight_sum(sides, start, length, split, received=(), ordered=False):
    kinds, places, rows = split
    parts = []
    for part in range(len(sides[0][1])):
        total = None
        for left, rights in sides:
            array, at, width = rights[part]
            term = over_tokens(left[:, start : start + length], array[:, at : at + width])
            total = term if total is None else total + term
        parts.append(total)
    groups = [group if isinstance(group, tuple) else (group,) for group in received]
    for pieces in zip(*groups):
        whole, at = jnp.concatenate(pieces, 0), 0
        for number, total in enumerate(parts):
            width = total.shape[1]
            parts[number] = total + whole[:, at : at + width].astype(jnp.float32)
            at += width
    whole = [total.astype(BF16) for total in parts]
    whole = jnp.concatenate(whole, 1) if len(whole) > 1 else whole[0]
    if not ordered:
        return jnp.split(whole, length // (places * rows), 0)
    cut = whole.reshape(length // (places * rows), places, rows, whole.shape[1])
    return jnp.transpose(cut, (1, 0, 2, 3))


def small_sums(lefts, rights, width):
    terms = [over_tokens(left, right).astype(BF16) for left, right in zip(lefts, rights)]
    used = sum(term.shape[1] for term in terms)
    if width > used:
        terms.append(jnp.zeros((terms[0].shape[0], width - used), BF16))
    return jnp.concatenate(terms, 1).reshape(-1, 2, width // 2)


def masked_scores(query_low, key_low, allowed, scale):
    raw = jnp.einsum("thd,sd->hts", query_low, key_low, preferred_element_type=jnp.float32)
    return jnp.where(allowed, raw * scale, -1e30)


def attend(query, key, value, cosine, sine, query_g, key_g, allowed, scale):
    count, dim = key.shape
    heads = query.reshape(count, -1, dim)
    query_low = rotate(rms_norm(heads, query_g), cosine, sine).astype(BF16)
    key_low = rotate(rms_norm(key[:, None], key_g), cosine, sine).astype(BF16)[:, 0]
    scores = masked_scores(query_low, key_low, allowed, scale)
    most = jnp.max(scores, -1, keepdims=True)
    log_total = most + jnp.log(jnp.sum(jnp.exp(scores - most), -1, keepdims=True))
    probs = jnp.exp(scores - log_total).astype(BF16)
    out = jnp.einsum("hts,sd->thd", probs, value, preferred_element_type=jnp.float32)
    return out.reshape(count, -1), query_low, key_low, log_total


def attend_back(
    d_out, query, key, query_low, key_low, value, lse, cosine, sine, query_g, key_g, allowed, scale
):
    count, dim = key.shape
    d_heads = d_out.astype(BF16).reshape(count, -1, dim)
    probs = jnp.exp(masked_scores(query_low, key_low, allowed, scale) - lse)
    d_probs = jnp.einsum("thd,sd->hts", d_heads, value, preferred_element_type=jnp.float32)
    inner = jnp.sum(probs * d_probs, -1, keepdims=True)
    d_scores = (probs * (d_probs - inner)).astype(BF16)
    d_query = jnp.einsum("hts,sd->thd", d_scores, key_low, preferred_element_type=jnp.float32)
    d_key = jnp.einsum("hts,thd->sd", d_scores, query_low, preferred_element_type=jnp.float32)
    d_value = jnp.einsum(
        "hts,thd->sd", probs.astype(BF16), d_heads, preferred_element_type=jnp.float32
    )
    d_query, d_query_g = norm_back(
        query.reshape(count, -1, dim), query_g, rotate_back(d_query * scale, cosine, sine)
    )
    d_key, d_key_g = norm_back(
        key[:, None], key_g, rotate_back((d_key * scale)[:, None], cosine, sine)
    )
    return d_query.reshape(count, -1), d_key[:, 0], d_value, d_query_g[None], d_key_g[None]


def paired_plan(
    tokens,
    layer_inputs,
    cotangent,
    doc_lengths,
    w_query,
    w_key,
    w_value,
    w_output,
    laurel_left,
    laurel_right,
    w_gate,
    w_up,
    w_down,
    w_plgate,
    w_plproj,
    g_input,
    g_query,
    g_key,
    g_attn,
    g_laurel,
    g_preffw,
    g_ffw,
    g_perlayer,
):
    f32 = jnp.float32
    batch_at = lax.axis_index("batch")
    y_at, x_at = batch_at // 2, batch_at % 2
    core = lax.axis_index("seq")
    depth = lax.axis_size("fsdp")
    shards = lax.axis_size("batch") * lax.axis_size("seq") * depth
    shard_at = (batch_at * 2 + core) * depth + lax.axis_index("fsdp")
    rows = w_query.shape[0]
    model = rows * shards
    half_model, quarter_model = model // 2, model // 4
    tok_rows = tokens.shape[1]
    seq_rows = 2 * tok_rows
    head_dim = g_query.shape[0] * shards
    head_part = g_query.shape[0]
    score_scale = head_dim ** (-0.5)
    rank, pl_width = laurel_left.shape[1], w_plgate.shape[1]
    ff_width = w_gate.shape[1]
    ff_part = ff_width // 4
    query_width, kv_width = w_query.shape[1] // 2, w_key.shape[1] // 2
    small_used = 2 * rank + 2 * pl_width
    small_width = -(-small_used // 256) * 256

    own_gains = jnp.stack([g_input, g_attn, g_laurel, g_preffw, g_ffw, g_perlayer]).astype(f32)
    head_gains = jnp.stack([g_query, g_key]).astype(f32)
    table = jnp.zeros((8, model), f32)
    table = lax.dynamic_update_slice(table, own_gains, (0, shard_at * rows))
    table = lax.dynamic_update_slice(table, head_gains, (6, shard_at * head_part))
    gain_table = sum_all(table)
    query_g, key_g = gain_table[6:7, :head_dim], gain_table[7:8, :head_dim]
    model_g = halves_by(y_at, gain_table[:6], 1)
    input_g, attn_g, laurel_g, preffw_g, ffw_g, perlayer_g = [model_g[i] for i in range(6)]

    def core_half(array):
        pair = array.reshape(rows, 2, -1)
        return pick(pair, 1, core), pick(pair, 1, 1 - core)

    def ff_block(array):
        parts = array.reshape(rows, 2, 2, ff_part)
        keep, send = pick(parts, 2, core), pick(parts, 2, 1 - core)
        both = in_order(core, keep, swap_core(send), 0)
        return pick(both, 2, x_at), pick(both, 2, 1 - x_at)

    def ff_exchange(keep, send):
        return in_order(x_at, keep, swap_x(send), 0).reshape(4, rows, ff_part)

    small_own = jnp.concatenate(
        [
            laurel_left,
            laurel_right,
            w_plgate,
            w_plproj,
            jnp.zeros((rows, small_width - small_used), BF16),
        ],
        1,
    )
    first_keep, first_send = zip(
        *[core_half(entry) for entry in (w_query, w_key, w_value, small_own)]
    )
    first_keep = jnp.concatenate(first_keep, 1)
    first_block = in_order(core, first_keep, swap_core(jnp.concatenate(first_send, 1)), 0)
    first_z = jnp.concatenate(gather_z(first_block), 0)
    out_keep, out_send = core_half(w_output)
    gate_four = ff_exchange(*ff_block(w_gate))
    up_keep, up_send = ff_block(w_up)
    up_four = ff_exchange(up_keep, after(up_send, gate_four))
    down_keep, down_send = ff_block(w_down)
    down_four = ff_exchange(down_keep, after(down_send, up_four))
    out_block = in_order(core, out_keep, swap_core(out_send), 0)
    gate_z = gather_z(after(gate_four, first_block))
    out_z = jnp.concatenate(gather_z(after(out_block, gate_four)), 0)
    up_z = gather_z(after(up_four, out_block))
    ff_half = ff_part // 2
    down_later = after(down_four[:, :, ff_half:], up_four)
    down_z = gather_z(down_later)
    down_early = down_four[:, :, :ff_half]
    down_both = jnp.concatenate([down_early, swap_y(down_early)], 0)
    down_eight = gather_z(after(down_both, down_later))

    resid_in = halves_by(y_at, tokens[0], 1).astype(f32)
    upstream = halves_by(y_at, cotangent[0], 1).astype(f32)
    perlayer = layer_inputs[0].astype(f32)
    own_places = core * tok_rows + jnp.arange(tok_rows, dtype=jnp.int32)
    other_places = (1 - core) * tok_rows + jnp.arange(tok_rows, dtype=jnp.int32)
    places = jnp.concatenate([own_places, other_places])
    segment, rel_pos = positions_of(places, doc_lengths[0])
    cosine, sine = rope_tables(rel_pos, head_dim)
    distance = places[:, None] - places[None, :]
    allowed = (
        (segment[:, None] == segment[None, :]) & (distance >= 0) & (distance < WINDOW)
    )

    def with_partner(own):
        return jnp.concatenate([own, swap_core(own)], 0)

    x_normed = rms_norm(resid_in, input_g)
    x_low = x_normed.astype(BF16)
    x_own_pairs = lax.optimization_barrier(to_pairs(x_at, x_low, 1))
    first_z = after(first_z, (down_both, gain_table))
    first_x, first_y = swap_x(first_z), swap_y(first_z)
    x_pairs, cosine, sine, upstream = lax.optimization_barrier(
        (with_partner(x_own_pairs), cosine, sine, upstream)
    )
    part = first_z.shape[0] // 2
    first_corner = [
        swap_y(after(first_x[:part], (x_pairs, cosine))),
        swap_x(after(first_y[part:], (x_pairs, cosine))),
    ]
    first_w = jnp.concatenate([first_z, first_y, first_x] + first_corner, 0)
    gate_far = chained(swap_y, gate_z, first_corner)

    query_raw = project(x_pairs, first_w[:, :query_width])
    key_raw = project(x_pairs, first_w[:, query_width : query_width + kv_width])
    value_low = project(
        x_pairs, first_w[:, query_width + kv_width : query_width + 2 * kv_width]
    ).astype(BF16)
    small_mine = first_w[:, query_width + 2 * kv_width :]
    small_mine = after(small_mine, query_raw)
    small_pair = in_order(core, small_mine, swap_core(small_mine), 0)
    small_all = from_pairs(x_at, jnp.concatenate([small_pair[0], small_pair[1]], 1), 0)
    left_w, right_w, plgate_w, plproj_w = split_columns(
        small_all, [rank, rank, pl_width, pl_width]
    )
    out_z = after(out_z, query_raw)
    query_raw = after(query_raw, gate_far[0])
    out_x, out_y = swap_x(out_z), swap_y(out_z)
    attn_heads, query_low, key_low, lse = attend(
        query_raw, key_raw, value_low, cosine, sine, query_g[0], key_g[0], allowed, score_scale
    )
    out_x, out_y, attn_heads = lax.optimization_barrier(
        (out_x, out_y, after(attn_heads, gate_far[1]))
    )
    attn_low = attn_heads.astype(BF16)
    out_corner = [swap_y(out_x[:part]), swap_x(out_y[part:])]
    output_w = jnp.concatenate([out_z, out_y, out_x] + out_corner, 0)
    up_far = chained(swap_y, up_z, gate_far)
    down_far = chained(swap_y, down_z, up_far)
    def side_by_side(early, late):
        whole = jnp.zeros((model, ff_part), BF16)
        whole = lax.dynamic_update_slice(whole, jnp.concatenate(early, 0), (0, 0))
        return lax.dynamic_update_slice(whole, jnp.concatenate(late, 0), (0, ff_half))

    left_low = project(x_low, left_w).astype(BF16)
    right_out = against_rows(left_low, right_w)
    attn_keep, attn_send = onto_model([attn_low], [output_w])
    attn_proj = from_pairs(x_at, attn_keep + swap_core(attn_send).astype(f32), 1)
    hidden = (
        resid_in + rms_norm(attn_proj, attn_g) + x_normed + rms_norm(right_out, laurel_g)
    ) * ROOT_HALF

    def sum_near_and_far(near_of, far):
        far_sum = (far[0] + swap_core(far[1]).astype(f32)).astype(BF16)
        crossed = swap_x(far_sum)
        near = near_of(far_sum)
        return near[0] + swap_core(near[1]).astype(f32), crossed, near

    ffw_in = rms_norm(hidden, preffw_g).astype(BF16)
    ffw_far = swap_x(ffw_in)
    ffw_near = with_partner(ffw_in)
    gate_w, up_w = [
        jnp.concatenate([after(mine[0], ffw_near)] + mine[1:] + far, 0)
        for mine, far in ((gate_z, gate_far), (up_z, up_far))
    ]
    gates_near, ups_near, act_near = gate_up_act(ffw_near, gate_w, up_w)
    ffw_far = with_partner(after(ffw_far, act_near))
    down_w = side_by_side([after(down_eight[0], act_near)] + down_eight[1:], down_z + down_far)
    gates_far, ups_far, act_far = gate_up_act(after(ffw_far, down_far[0]), gate_w, up_w)
    downs_far = onto_model([act_far], [down_w])
    down_terms, crossed, _ = sum_near_and_far(
        lambda earlier: onto_model([after(act_near, earlier)], [down_w]), downs_far
    )
    down_terms = down_terms + crossed.astype(f32)
    second = hidden + rms_norm(down_terms, ffw_g)
    second_low = second.astype(BF16)
    plgate_out = project(second_low, plgate_w)
    gated_low = geglu(plgate_out, perlayer).astype(BF16)
    plproj_out = against_rows(gated_low, plproj_w)
    mixed_out = halves_by(y_at, (second + rms_norm(plproj_out, perlayer_g)).astype(BF16), 1)

    d_plproj, d_perlayer_g = norm_back(plproj_out, perlayer_g, upstream)
    d_plproj_low = d_plproj.astype(BF16)
    d_gated = project(d_plproj_low, plproj_w)
    d_plgate_low = jax.vjp(geglu, plgate_out, perlayer)[1](d_gated)[0].astype(BF16)
    d_second = upstream + against_rows(d_plgate_low, plgate_w)
    d_down, d_ffw_g = norm_back(down_terms, ffw_g, d_second)
    d_down_low = d_down.astype(BF16)
    d_down_far = swap_x(d_down_low)
    d_down_near = with_partner(d_down_low)
    d_gate_near, d_up_near = gate_up_back(d_down_near, down_w, gates_near, ups_near)
    d_down_far = with_partner(after(d_down_far, d_gate_near))

    ff_split = (4, depth, rows)

    def ff_send(sides, first_column=0, width=ff_part):
        cut = [(left, [(right, first_column, width)]) for left, right in sides]
        return weight_sum(cut, half_model, half_model, ff_split)

    def ff_keep(sides, received, first_column=0, width=ff_part):
        cut = [(left, [(right, first_column, width)]) for left, right in sides]
        return weight_sum(cut, 0, half_model, ff_split, received, True)

    def ff_owned(four):
        four = four.reshape(2, 2, rows, ff_part)
        keep, send = pick(four, 0, x_at), pick(four, 0, 1 - x_at)
        over = swap_x(send)
        a, b = pick(keep, 0, core), pick(over, 0, core)
        crossed = swap_core(jnp.stack([pick(keep, 0, 1 - core), pick(over, 0, 1 - core)]))
        quarters = []
        for x_of in range(2):
            near = jnp.where(x_at == x_of, a, b)
            far = jnp.where(x_at == x_of, crossed[0], crossed[1])
            quarters += [
                jnp.where(core == c_of, near, far).astype(f32) for c_of in range(2)
            ]
        return jnp.concatenate(quarters, 1)

    down_sides = [(d_down_near, act_near), (d_down_far, act_far)]
    down_sent = ff_send(down_sides, ff_half, ff_half)
    down_near = chained(swap_y, down_sent)
    whole_cut = [(left, [(right, 0, ff_half)]) for left, right in down_sides]
    down_whole = weight_sum(whole_cut, 0, model, (8, depth, rows), (), True)
    down_eight = scatter_z(down_whole)
    d_gate_far, d_up_far = gate_up_back(
        d_down_far, down_w, after(gates_far, down_near[0]), ups_far
    )
    gate_sides = [(ffw_near, d_gate_near), (ffw_far, d_gate_far)]
    up_sides = [(ffw_near, d_up_near), (ffw_far, d_up_far)]
    ffw_weights = [gate_w, up_w]
    gate_sent = ff_send(gate_sides)
    gate_near = chained(swap_y, gate_sent, down_near)
    d_ffw_far = onto_model([d_gate_far, d_up_far], ffw_weights)
    d_ffw_terms, crossed, d_ffw_near = sum_near_and_far(
        lambda earlier: onto_model(
            [after(d_gate_near, (earlier, gate_near[0], down_eight)), d_up_near], ffw_weights
        ),
        d_ffw_far,
    )
    up_sent = ff_send(up_sides)
    up_near = chained(swap_y, up_sent, gate_near)
    down_near = [after(down_near[0], up_sent)] + down_near[1:]
    down_kept = ff_keep(down_sides, down_near, ff_half, ff_half)
    down_four = scatter_z(down_kept)
    gate_near = [after(gate_near[0], down_kept)] + gate_near[1:]
    gate_kept = ff_keep(gate_sides, gate_near)
    gate_four = scatter_z(gate_kept)
    d_ffw_terms = d_ffw_terms + after(crossed, gate_kept).astype(f32)

    d_hidden_norm, d_preffw_g = norm_back(hidden, preffw_g, d_ffw_terms)
    d_branch = (d_second + d_hidden_norm) * ROOT_HALF
    d_laurel, d_laurel_g = norm_back(right_out, laurel_g, d_branch)
    d_laurel_low = d_laurel.astype(BF16)
    d_left_low = project(d_laurel_low, right_w).astype(BF16)
    d_attn, d_attn_g = norm_back(attn_proj, attn_g, d_branch)
    d_attn_pairs = with_partner(lax.optimization_barrier(to_pairs(x_at, d_attn.astype(BF16), 1)))

    pair_split = (2, depth, rows)

    def whole_columns(keep, received):
        ends = [jnp.where(core == c_of, keep, received).astype(f32) for c_of in range(2)]
        return jnp.concatenate(ends, 1)

    def pair_owned(pair):
        pair = pair.reshape(2, rows, pair.shape[1])
        keep, send = pick(pair, 0, core), pick(pair, 0, 1 - core)
        return keep, swap_core(send)

    def pair_send(sides):
        return weight_sum(sides, half_model, half_model, pair_split)

    def pair_pass(sides, over_x):
        return weight_sum(sides, quarter_model, quarter_model, pair_split, over_x[2:])

    def pair_keep(sides, over_x, over_y):
        got = list(zip(over_x[:2], over_y))
        return weight_sum(sides, 0, quarter_model, pair_split, got, True)

    out_sides = [(d_attn_pairs, [(attn_low, 0, query_width)])]
    out_sent = pair_send(out_sides)
    out_near = chained(swap_x, out_sent[2:] + out_sent[:2])
    out_near = out_near[2:] + out_near[:2]
    d_heads = project(d_attn_pairs, output_w)
    d_heads = after(d_heads, (up_near[1], down_four))
    d_query_low, d_key_low, d_value_low, d_query_g, d_key_g = attend_back(
        d_heads,
        query_raw,
        key_raw,
        query_low,
        key_low,
        value_low,
        lse,
        cosine,
        sine,
        query_g[0],
        key_g[0],
        allowed,
        score_scale,
    )

    d_query_low, d_key_low, d_value_low = [
        entry.astype(BF16) for entry in (d_query_low, d_key_low, d_value_low)
    ]
    first_rights = [
        (d_query_low, 0, query_width),
        (d_key_low, 0, kv_width),
        (d_value_low, 0, kv_width),
    ]
    first_sides = [(x_pairs, first_rights)]
    first_sent = pair_send(first_sides)
    first_near = chained(swap_x, first_sent[2:] + first_sent[:2], out_near[:2])
    first_near = first_near[2:] + first_near[:2]
    up_kept = ff_keep(up_sides, up_near)
    up_four = scatter_z(up_kept)
    small_halves = small_sums(
        [x_low, d_laurel_low, second_low, d_plproj_low],
        [d_left_low, left_low, d_plgate_low, gated_low],
        small_width,
    )
    small_sum = pick(small_halves, 1, core).astype(f32) + swap_core(
        pick(small_halves, 1, 1 - core)
    ).astype(f32)
    small_sum = small_sum.astype(BF16).reshape(2, 2, quarter_model, small_width // 2)
    over_x = swap_x(pick(small_sum, 1, 1 - x_at))
    small_sum = pick(small_sum, 1, x_at).astype(f32) + over_x.astype(f32)
    small_sum = small_sum[0] + swap_y(small_sum[1].astype(BF16)).astype(f32)
    small_sum = small_sum.reshape(2, depth, rows, small_width // 2).astype(BF16)
    small_pair = scatter_z_small(jnp.transpose(small_sum, (1, 0, 2, 3)))
    small_keep, small_send = pick(small_pair, 0, core), pick(small_pair, 0, 1 - core)
    out_right = out_sides[0][1]
    out_near = out_near[:2] + [after(out_near[2], up_kept), out_near[3]]
    out_passed = pair_pass([(d_attn_pairs, out_right)], out_near)
    out_over = chained(swap_y, out_passed, up_near)
    first_w_parts = split_columns(
        first_w[:, : query_width + 2 * kv_width], [query_width, kv_width, kv_width]
    )
    d_x_keep, d_x_send = onto_model([d_query_low, d_key_low, d_value_low], first_w_parts)
    d_x_terms = from_pairs(x_at, d_x_keep + swap_core(d_x_send).astype(f32), 1)
    d_x_terms = d_x_terms + against_rows(d_left_low, left_w)
    d_input, d_input_g = norm_back(resid_in, input_g, d_x_terms + d_branch)
    grad_tokens = halves_by(y_at, d_input + d_branch, 1)[None]

    widths = [query_width, kv_width, kv_width]
    first_passed = pair_pass([(x_pairs, first_rights)], first_near)
    first_over = chained(swap_y, first_passed, out_over)
    out_over = [after(out_over[0], up_four)] + out_over[1:]
    out_kept = pair_keep([(d_attn_pairs, out_right)], out_near, out_over)
    out_four = scatter_z(out_kept)
    first_kept = pair_keep([(x_pairs, first_rights)], first_near, first_over)
    first_four = scatter_z(first_kept)
    grad_output = whole_columns(*pair_owned(out_four))
    first_keep, first_received = pair_owned(first_four)
    grad_query, grad_key, grad_value = [
        whole_columns(keep, received)
        for keep, received in zip(
            split_columns(first_keep, widths), split_columns(first_received, widths)
        )
    ]

    grad_left, grad_right, grad_plgate, grad_plproj = split_columns(
        whole_columns(small_keep, swap_core(small_send)), [rank, rank, pl_width, pl_width]
    )

    down_eight, down_four = after((down_eight, down_four), d_query_low)
    down_eight = down_eight.reshape(2, 4, rows, ff_half)
    down_last = down_eight[0].astype(f32) + swap_y(down_eight[1]).astype(f32)
    grad_down = ff_owned(
        jnp.concatenate([down_last.astype(BF16), down_four.reshape(4, rows, ff_half)], 2)
    )
    grad_gate = ff_owned(after(gate_four, out_passed))
    grad_up = ff_owned(up_four)

    gain_grads = jnp.stack(
        [d_input_g, d_attn_g, d_laurel_g, d_preffw_g, d_ffw_g, d_perlayer_g]
    )
    head_grads = jnp.pad(
        jnp.concatenate([d_query_g, d_key_g], 0), ((0, 0), (0, model - head_dim))
    )
    gain_sums = sum_all(jnp.concatenate([halves_by(y_at, gain_grads, 1), head_grads], 0))
    own_sums = lax.dynamic_slice(gain_sums, (0, shard_at * rows), (6, rows))
    own_heads = lax.dynamic_slice(gain_sums, (6, shard_at * head_part), (2, head_part))
    (
        grad_g_input,
        grad_g_attn,
        grad_g_laurel,
        grad_g_preffw,
        grad_g_ffw,
        grad_g_perlayer,
    ) = [own_sums[i] for i in range(6)]
    grad_g_query, grad_g_key = own_heads[0], own_heads[1]
    return (
        mixed_out[None],
        grad_tokens,
        grad_query,
        grad_key,
        grad_value,
        grad_output,
        grad_left,
        grad_right,
        grad_gate,
        grad_up,
        grad_down,
        grad_plgate,
        grad_plproj,
        grad_g_input,
        grad_g_query,
        grad_g_key,
        grad_g_attn,
        grad_g_laurel,
        grad_g_preffw,
        grad_g_ffw,
        grad_g_perlayer,
    )


def solution(mesh):
    paired = mesh.shape["batch"] == 4 and mesh.shape["seq"] == 2
    by_token = P(ROW_AXES, "seq", None)
    by_row = P(ALL_AXES, None)
    by_entry = P(ALL_AXES)
    return jax.shard_map(
        paired_plan if paired else whole_gather_plan,
        mesh=mesh,
        in_specs=(by_token,) * 3 + (P(ROW_AXES, None),) + (by_row,) * 11 + (by_entry,) * 8,
        out_specs=(by_token,) * 2 + (by_row,) * 11 + (by_entry,) * 8,
        check_vma=False,
    )
```

```python
import jax
import jax.numpy as jnp
from jax import lax
from jax.sharding import PartitionSpec as P

WINDOW = 512
ALL_AXES = ("batch", "seq", "fsdp")
ROW_AXES = ("batch", "fsdp")


EPS = 1e-06
THETA = 10000.0
ROOT_HALF = 0.7071067811865476


def shifted(array, axis, by):
    count = lax.axis_size(axis)
    pairs = [(i, i + by) for i in range(count) if 0 <= i + by < count]
    return lax.ppermute(array, axis, pairs)


def rms_norm(values, weight):
    return values * lax.rsqrt(jnp.mean(values * values, -1, keepdims=True) + EPS) * weight


def norm_back(values, weight, upstream):
    normed, pull = jax.vjp(rms_norm, values, weight)
    return pull(upstream)


def geglu(gate_in, factor):
    return jax.nn.gelu(gate_in, approximate=True) * factor


def positions_of(places, lengths):
    doc_ends = jnp.cumsum(lengths)
    starts = doc_ends - lengths
    segment = jnp.sum((places[:, None] >= doc_ends[None, :]).astype(jnp.int32), 1)
    chosen = segment[:, None] == jnp.arange(lengths.shape[0], dtype=jnp.int32)[None, :]
    offset = jnp.sum(jnp.where(chosen, starts[None, :], 0), 1)
    return (segment, (places - offset).astype(jnp.float32))


def rope_tables(rel_pos, width_all):
    half_width = width_all // 2
    frequency = THETA ** (-jnp.arange(half_width, dtype=jnp.float32) * 2.0 / width_all)
    angles = rel_pos[:, None] * frequency[None, :]
    return (jnp.cos(angles)[:, None, :], jnp.sin(angles)[:, None, :])


def rotate(values, cosine_table, sine_table):
    half_width = values.shape[-1] // 2
    leading = values[..., :half_width]
    trailing = values[..., half_width:]
    return jnp.concatenate(
        [
            leading * cosine_table - trailing * sine_table,
            trailing * cosine_table + leading * sine_table,
        ],
        -1,
    )


def rotate_back(upstream, cosine_table, sine_table):
    half_width = upstream.shape[-1] // 2
    leading = upstream[..., :half_width]
    trailing = upstream[..., half_width:]
    return jnp.concatenate(
        [
            leading * cosine_table + trailing * sine_table,
            trailing * cosine_table - leading * sine_table,
        ],
        -1,
    )


def project(left, right):
    return jnp.dot(left, right, preferred_element_type=jnp.float32)


def against_rows(left, right):
    return lax.dot_general(
        left, right, (((1,), (1,)), ((), ())), preferred_element_type=jnp.float32
    )


def over_tokens(left, right):
    return lax.dot_general(
        left, right, (((0,), (0,)), ((), ())), preferred_element_type=jnp.float32
    )


def split_columns(packed, widths):
    pieces = []
    column_at = 0
    for width_one in widths:
        pieces.append(packed[:, column_at : column_at + width_one])
        column_at = column_at + width_one
    return pieces


def whole_gather_plan(
    tokens,
    layer_inputs,
    cotangent,
    doc_lengths,
    w_query,
    w_key,
    w_value,
    w_output,
    laurel_left,
    laurel_right,
    w_gate,
    w_up,
    w_down,
    w_plgate,
    w_plproj,
    g_input,
    g_query,
    g_key,
    g_attn,
    g_laurel,
    g_preffw,
    g_ffw,
    g_perlayer,
):
    gathered = (
        lax.all_gather(w_query, ALL_AXES, axis=0, tiled=True),
        lax.all_gather(w_key, ALL_AXES, axis=0, tiled=True),
        lax.all_gather(w_value, ALL_AXES, axis=0, tiled=True),
        lax.all_gather(w_output, ALL_AXES, axis=0, tiled=True),
        lax.all_gather(laurel_left, ALL_AXES, axis=0, tiled=True),
        lax.all_gather(laurel_right, ALL_AXES, axis=0, tiled=True),
        lax.all_gather(w_gate, ALL_AXES, axis=0, tiled=True),
        lax.all_gather(w_up, ALL_AXES, axis=0, tiled=True),
        lax.all_gather(w_down, ALL_AXES, axis=0, tiled=True),
        lax.all_gather(w_plgate, ALL_AXES, axis=0, tiled=True),
        lax.all_gather(w_plproj, ALL_AXES, axis=0, tiled=True),
        lax.all_gather(g_input, ALL_AXES, axis=0, tiled=True),
        lax.all_gather(g_query, ALL_AXES, axis=0, tiled=True),
        lax.all_gather(g_key, ALL_AXES, axis=0, tiled=True),
        lax.all_gather(g_attn, ALL_AXES, axis=0, tiled=True),
        lax.all_gather(g_laurel, ALL_AXES, axis=0, tiled=True),
        lax.all_gather(g_preffw, ALL_AXES, axis=0, tiled=True),
        lax.all_gather(g_ffw, ALL_AXES, axis=0, tiled=True),
        lax.all_gather(g_perlayer, ALL_AXES, axis=0, tiled=True),
    )
    query_w, key_w, value_w, output_w, left_w, right_w, gate_w, up_w, down_w, plgate_w, plproj_w = (
        gathered[:11]
    )
    input_g, query_g, key_g, attn_g, laurel_g, preffw_g, ffw_g, perlayer_g = [
        entry.astype(jnp.float32) for entry in gathered[11:]
    ]
    head_dim = query_g.shape[0]
    num_heads = query_w.shape[1] // head_dim
    kv_heads = key_w.shape[1] // head_dim
    groups = num_heads // kv_heads
    width_kv = kv_heads * head_dim
    score_scale = head_dim ** (-0.5)
    seq_pos = lax.axis_index("seq")
    tok_rows = tokens.shape[1]
    reach_hops = min((WINDOW - 2) // tok_rows + 1, lax.axis_size("seq") - 1)
    resid_in = tokens[0].astype(jnp.float32)
    perlayer = layer_inputs[0].astype(jnp.float32)
    upstream = cotangent[0].astype(jnp.float32)
    lengths = doc_lengths[0]
    places = seq_pos * tok_rows + jnp.arange(tok_rows, dtype=jnp.int32)
    segment, rel_pos = positions_of(places, lengths)
    cosine_table, sine_table = rope_tables(rel_pos, head_dim)
    ff_width = gate_w.shape[1]
    x_normed = rms_norm(resid_in, input_g)
    x_low = x_normed.astype(jnp.bfloat16)
    query_heads = project(x_low, query_w).reshape(tok_rows, num_heads, head_dim)
    key_heads = project(x_low, key_w).reshape(tok_rows, kv_heads, head_dim)
    value_raw = project(x_low, value_w)
    query_low = rotate(rms_norm(query_heads, query_g), cosine_table, sine_table).astype(
        jnp.bfloat16
    )
    key_rot = rotate(rms_norm(key_heads, key_g), cosine_table, sine_table)
    kv_local = jnp.concatenate([key_rot.reshape(tok_rows, width_kv), value_raw], 1).astype(
        jnp.bfloat16
    )
    pieces = []
    for distance in range(reach_hops, 0, -1):
        pieces.append(shifted(kv_local, "seq", distance))
    kv_window = jnp.concatenate(pieces + [kv_local], 0)
    key_places = (seq_pos - reach_hops) * tok_rows + jnp.arange(
        (reach_hops + 1) * tok_rows, dtype=jnp.int32
    )
    key_segment, key_rel = positions_of(key_places, lengths)
    distance_all = places[:, None] - key_places[None, :]
    allowed = (
        (segment[:, None] == key_segment[None, :])
        & (distance_all >= 0)
        & (distance_all < WINDOW)
        & (key_places[None, :] >= 0)
    )
    keys_win = kv_window[:, :width_kv].reshape(-1, kv_heads, head_dim)
    values_win = kv_window[:, width_kv:].reshape(-1, kv_heads, head_dim)
    query_group = query_low.reshape(tok_rows, kv_heads, groups, head_dim)

    def scores_of():
        raw_scores = (
            jnp.einsum("tkgd,skd->kgts", query_group, keys_win, preferred_element_type=jnp.float32)
            * score_scale
        )
        return jnp.where(allowed, raw_scores, -1e30)

    scores = scores_of()
    row_max = jnp.max(scores, -1, keepdims=True)
    row_total = jnp.sum(jnp.exp(scores - row_max), -1, keepdims=True)
    log_total = row_max + jnp.log(row_total)
    attn_probs = jnp.exp(scores - log_total)
    attn_heads = jnp.einsum(
        "kgts,skd->tkgd",
        attn_probs.astype(jnp.bfloat16),
        values_win,
        preferred_element_type=jnp.float32,
    )
    attn_low = attn_heads.reshape(tok_rows, num_heads * head_dim).astype(jnp.bfloat16)
    attn_proj = against_rows(attn_low, output_w)
    left_low = project(x_low, left_w).astype(jnp.bfloat16)
    right_out = against_rows(left_low, right_w)
    hidden = (
        resid_in + rms_norm(attn_proj, attn_g) + x_normed + rms_norm(right_out, laurel_g)
    ) * ROOT_HALF
    ffw_in = rms_norm(hidden, preffw_g).astype(jnp.bfloat16)
    gate_used, up_used, down_used = (gate_w, up_w, down_w)
    gate_out = project(ffw_in, gate_used)
    up_out = project(ffw_in, up_used)
    act_low = geglu(gate_out, up_out).astype(jnp.bfloat16)
    down_terms = against_rows(act_low, down_used)
    second = hidden + rms_norm(down_terms, ffw_g)
    second_low = second.astype(jnp.bfloat16)
    plgate_out = project(second_low, plgate_w)
    gated_low = geglu(plgate_out, perlayer).astype(jnp.bfloat16)
    plproj_out = against_rows(gated_low, plproj_w)
    mixed_out = (second + rms_norm(plproj_out, perlayer_g)).astype(jnp.bfloat16)
    d_plproj, d_perlayer_g = norm_back(plproj_out, perlayer_g, upstream)
    d_plproj_low = d_plproj.astype(jnp.bfloat16)
    d_gated = project(d_plproj_low, plproj_w)
    d_plgate_low = jax.vjp(geglu, plgate_out, perlayer)[1](d_gated)[0].astype(jnp.bfloat16)
    d_second = upstream + against_rows(d_plgate_low, plgate_w)
    d_down, d_ffw_g = norm_back(down_terms, ffw_g, d_second)
    d_down_low = d_down.astype(jnp.bfloat16)
    d_act = project(d_down_low, down_used)
    d_gate, d_up = jax.vjp(geglu, gate_out, up_out)[1](d_act)
    d_gate_low = d_gate.astype(jnp.bfloat16)
    d_up_low = d_up.astype(jnp.bfloat16)
    d_ffw_terms = against_rows(d_gate_low, gate_used) + against_rows(d_up_low, up_used)
    d_hidden_norm, d_preffw_g = norm_back(hidden, preffw_g, d_ffw_terms)
    d_branch = (d_second + d_hidden_norm) * ROOT_HALF
    ffn_grads = lax.psum_scatter(
        jnp.concatenate(
            [
                over_tokens(ffw_in, d_gate_low),
                over_tokens(ffw_in, d_up_low),
                over_tokens(d_down_low, act_low),
            ],
            1,
        ),
        ALL_AXES,
        scatter_dimension=0,
        tiled=True,
    )
    d_laurel, d_laurel_g = norm_back(right_out, laurel_g, d_branch)
    d_laurel_low = d_laurel.astype(jnp.bfloat16)
    d_left_low = project(d_laurel_low, right_w).astype(jnp.bfloat16)
    d_attn, d_attn_g = norm_back(attn_proj, attn_g, d_branch)
    d_attn_low = d_attn.astype(jnp.bfloat16)
    d_heads = project(d_attn_low, output_w).astype(jnp.bfloat16)
    d_group = d_heads.reshape(tok_rows, kv_heads, groups, head_dim)
    scores = scores_of()
    attn_probs = jnp.exp(scores - log_total)
    d_probs = jnp.einsum("tkgd,skd->kgts", d_group, values_win, preferred_element_type=jnp.float32)
    d_scores = (attn_probs * (d_probs - jnp.sum(attn_probs * d_probs, -1, keepdims=True))).astype(
        jnp.bfloat16
    )
    d_query_rot = (
        jnp.einsum("kgts,skd->tkgd", d_scores, keys_win, preferred_element_type=jnp.float32)
        * score_scale
    )
    d_keys = (
        jnp.einsum("kgts,tkgd->skd", d_scores, query_group, preferred_element_type=jnp.float32)
        * score_scale
    )
    d_values = jnp.einsum(
        "kgts,tkgd->skd",
        attn_probs.astype(jnp.bfloat16),
        d_group,
        preferred_element_type=jnp.float32,
    )
    d_kv = jnp.concatenate([d_keys.reshape(-1, width_kv), d_values.reshape(-1, width_kv)], 1)
    d_kv_local = d_kv[reach_hops * tok_rows :]
    for distance in range(reach_hops, 0, -1):
        piece_grad = d_kv[
            (reach_hops - distance) * tok_rows : (reach_hops - distance + 1) * tok_rows
        ]
        d_kv_local = d_kv_local + shifted(piece_grad.astype(jnp.bfloat16), "seq", -distance).astype(
            piece_grad.dtype
        )
    d_key_rot = d_kv_local[:, :width_kv].reshape(tok_rows, kv_heads, head_dim)
    d_value_low = d_kv_local[:, width_kv:].astype(jnp.bfloat16)
    d_query_norm = rotate_back(
        d_query_rot.reshape(tok_rows, num_heads, head_dim), cosine_table, sine_table
    )
    d_query_raw, d_query_g = norm_back(query_heads, query_g, d_query_norm)
    d_key_norm = rotate_back(d_key_rot, cosine_table, sine_table)
    d_key_raw, d_key_g = norm_back(key_heads, key_g, d_key_norm)
    d_query_low = d_query_raw.reshape(tok_rows, num_heads * head_dim).astype(jnp.bfloat16)
    d_key_low = d_key_raw.reshape(tok_rows, width_kv).astype(jnp.bfloat16)
    d_x_low = (
        against_rows(d_query_low, query_w)
        + against_rows(d_key_low, key_w)
        + against_rows(d_value_low, value_w)
        + against_rows(d_left_low, left_w)
    )
    d_input, d_input_g = norm_back(resid_in, input_g, d_x_low + d_branch)
    grad_tokens = (d_input + d_branch)[None]
    other_grads = lax.psum_scatter(
        jnp.concatenate(
            [
                over_tokens(x_low, d_query_low),
                over_tokens(x_low, d_key_low),
                over_tokens(x_low, d_value_low),
                over_tokens(d_attn_low, attn_low),
                over_tokens(x_low, d_left_low),
                over_tokens(d_laurel_low, left_low),
                over_tokens(second_low, d_plgate_low),
                over_tokens(d_plproj_low, gated_low),
            ],
            1,
        ),
        ALL_AXES,
        scatter_dimension=0,
        tiled=True,
    )
    other_widths = [
        query_w.shape[1],
        key_w.shape[1],
        value_w.shape[1],
        output_w.shape[1],
        left_w.shape[1],
        right_w.shape[1],
        plgate_w.shape[1],
        plproj_w.shape[1],
    ]
    (
        grad_query,
        grad_key,
        grad_value,
        grad_output,
        grad_left,
        grad_right,
        grad_plgate,
        grad_plproj,
    ) = split_columns(other_grads, other_widths)
    grad_gate, grad_up, grad_down = split_columns(ffn_grads, [ff_width, ff_width, ff_width])
    (
        grad_g_input,
        grad_g_query,
        grad_g_key,
        grad_g_attn,
        grad_g_laurel,
        grad_g_preffw,
        grad_g_ffw,
        grad_g_perlayer,
    ) = (
        lax.psum_scatter(d_input_g, ALL_AXES, scatter_dimension=0, tiled=True),
        lax.psum_scatter(d_query_g, ALL_AXES, scatter_dimension=0, tiled=True),
        lax.psum_scatter(d_key_g, ALL_AXES, scatter_dimension=0, tiled=True),
        lax.psum_scatter(d_attn_g, ALL_AXES, scatter_dimension=0, tiled=True),
        lax.psum_scatter(d_laurel_g, ALL_AXES, scatter_dimension=0, tiled=True),
        lax.psum_scatter(d_preffw_g, ALL_AXES, scatter_dimension=0, tiled=True),
        lax.psum_scatter(d_ffw_g, ALL_AXES, scatter_dimension=0, tiled=True),
        lax.psum_scatter(d_perlayer_g, ALL_AXES, scatter_dimension=0, tiled=True),
    )
    return (
        mixed_out[None],
        grad_tokens,
        grad_query,
        grad_key,
        grad_value,
        grad_output,
        grad_left,
        grad_right,
        grad_gate,
        grad_up,
        grad_down,
        grad_plgate,
        grad_plproj,
        grad_g_input,
        grad_g_query,
        grad_g_key,
        grad_g_attn,
        grad_g_laurel,
        grad_g_preffw,
        grad_g_ffw,
        grad_g_perlayer,
    )


BF16 = jnp.bfloat16
X_PAIRS = [(0, 1), (1, 0), (2, 3), (3, 2)]
Y_PAIRS = [(0, 2), (2, 0), (1, 3), (3, 1)]
CORE_PAIRS = [(0, 1), (1, 0)]


def swap_x(array):
    return lax.ppermute(array, "batch", X_PAIRS)


def swap_y(array):
    return lax.ppermute(array, "batch", Y_PAIRS)


def swap_core(array):
    return lax.ppermute(array, "seq", CORE_PAIRS)


def chained(swap, pieces, earlier=()):
    there = list(earlier)
    for piece in pieces:
        there.append(swap(after(piece, there[-2]) if len(there) > 1 else piece))
    return there[len(earlier) :]


def pick(array, axis, index):
    return lax.dynamic_index_in_dim(array, index, axis, keepdims=False)


def in_order(index, mine, theirs, axis):
    first = jnp.where(index == 0, mine, theirs)
    second = jnp.where(index == 0, theirs, mine)
    return jnp.stack([first, second], axis)


def halves_by(index, array, axis):
    low, high = jnp.split(array, 2, axis)
    return jnp.concatenate(
        [jnp.where(index == 0, low, high), jnp.where(index == 0, high, low)], axis
    )


def to_pairs(x_at, array, axis):
    b0, b1, b2, b3 = jnp.split(array, 4, axis)
    even = x_at == 0
    return jnp.concatenate(
        [
            jnp.where(even, b0, b1),
            jnp.where(even, b2, b3),
            jnp.where(even, b1, b0),
            jnp.where(even, b3, b2),
        ],
        axis,
    )


def from_pairs(x_at, array, axis):
    e0, e1, e2, e3 = jnp.split(array, 4, axis)
    even = x_at == 0
    return jnp.concatenate(
        [
            jnp.where(even, e0, e2),
            jnp.where(even, e2, e0),
            jnp.where(even, e1, e3),
            jnp.where(even, e3, e1),
        ],
        axis,
    )


def after(array, earlier):
    return lax.optimization_barrier((array, earlier))[0]


def gather_z(array):
    kinds, rows, width = array.shape
    stacked = lax.all_gather(array, "fsdp", axis=0, tiled=False)
    return [stacked[:, kind].reshape(-1, width) for kind in range(kinds)]


def scatter_z(ordered):
    count, kinds, rows, width = ordered.shape
    flat = ordered.reshape(count * kinds * rows, width)
    return lax.psum_scatter(flat, "fsdp", scatter_dimension=0, tiled=True)


def scatter_z_small(ordered):
    count = lax.axis_size("fsdp")
    z_at = lax.axis_index("fsdp")
    total = pick(ordered, 0, z_at).astype(jnp.float32)
    for by in range(1, count):
        turn = [(i, (i + by) % count) for i in range(count)]
        sent = pick(ordered, 0, lax.rem(z_at + by, count))
        total = total + lax.ppermute(sent, "fsdp", turn).astype(jnp.float32)
    return total.astype(BF16)


def sum_all(array):
    array = array + swap_core(array)
    array = array + swap_x(array)
    array = array + swap_y(array)
    count = lax.axis_size("fsdp")
    turns = [
        lax.ppermute(array, "fsdp", [(i, (i + by) % count) for i in range(count)])
        for by in range(1, count)
    ]
    return sum(turns, array)


def gate_up_act(left, gate_w, up_w):
    gate, up = project(left, gate_w), project(left, up_w)
    return gate.astype(BF16), up.astype(BF16), geglu(gate, up).astype(BF16)


def gate_up_back(left, down_w, gate, up):
    gate, up = gate.astype(jnp.float32), up.astype(jnp.float32)
    d_gate, d_up = jax.vjp(geglu, gate, up)[1](project(left, down_w))
    return d_gate.astype(BF16), d_up.astype(BF16)


def onto_model(lefts, weights):
    half = lefts[0].shape[0] // 2

    def total(cut):
        terms = [against_rows(left[cut], weight) for left, weight in zip(lefts, weights)]
        return sum(terms[1:], terms[0])

    return total(slice(0, half)), total(slice(half, None)).astype(BF16)


def weight_sum(sides, start, length, split, received=(), ordered=False):
    kinds, places, rows = split
    parts = []
    for part in range(len(sides[0][1])):
        total = None
        for left, rights in sides:
            array, at, width = rights[part]
            term = over_tokens(left[:, start : start + length], array[:, at : at + width])
            total = term if total is None else total + term
        parts.append(total)
    groups = [group if isinstance(group, tuple) else (group,) for group in received]
    for pieces in zip(*groups):
        whole, at = jnp.concatenate(pieces, 0), 0
        for number, total in enumerate(parts):
            width = total.shape[1]
            parts[number] = total + whole[:, at : at + width].astype(jnp.float32)
            at += width
    whole = [total.astype(BF16) for total in parts]
    whole = jnp.concatenate(whole, 1) if len(whole) > 1 else whole[0]
    if not ordered:
        return jnp.split(whole, length // (places * rows), 0)
    cut = whole.reshape(length // (places * rows), places, rows, whole.shape[1])
    return jnp.transpose(cut, (1, 0, 2, 3))


def small_sums(lefts, rights, width):
    terms = [over_tokens(left, right).astype(BF16) for left, right in zip(lefts, rights)]
    used = sum(term.shape[1] for term in terms)
    if width > used:
        terms.append(jnp.zeros((terms[0].shape[0], width - used), BF16))
    return jnp.concatenate(terms, 1).reshape(-1, 2, width // 2)


def masked_scores(query_low, key_low, allowed, scale):
    raw = jnp.einsum("thd,sd->hts", query_low, key_low, preferred_element_type=jnp.float32)
    return jnp.where(allowed, raw * scale, -1e30)


def attend(query, key, value, cosine, sine, query_g, key_g, allowed, scale):
    count, dim = key.shape
    heads = query.reshape(count, -1, dim)
    query_low = rotate(rms_norm(heads, query_g), cosine, sine).astype(BF16)
    key_low = rotate(rms_norm(key[:, None], key_g), cosine, sine).astype(BF16)[:, 0]
    scores = masked_scores(query_low, key_low, allowed, scale)
    most = jnp.max(scores, -1, keepdims=True)
    log_total = most + jnp.log(jnp.sum(jnp.exp(scores - most), -1, keepdims=True))
    probs = jnp.exp(scores - log_total).astype(BF16)
    out = jnp.einsum("hts,sd->thd", probs, value, preferred_element_type=jnp.float32)
    return out.reshape(count, -1), query_low, key_low, log_total


def attend_back(
    d_out, query, key, query_low, key_low, value, lse, cosine, sine, query_g, key_g, allowed, scale
):
    count, dim = key.shape
    d_heads = d_out.astype(BF16).reshape(count, -1, dim)
    probs = jnp.exp(masked_scores(query_low, key_low, allowed, scale) - lse)
    d_probs = jnp.einsum("thd,sd->hts", d_heads, value, preferred_element_type=jnp.float32)
    inner = jnp.sum(probs * d_probs, -1, keepdims=True)
    d_scores = (probs * (d_probs - inner)).astype(BF16)
    d_query = jnp.einsum("hts,sd->thd", d_scores, key_low, preferred_element_type=jnp.float32)
    d_key = jnp.einsum("hts,thd->sd", d_scores, query_low, preferred_element_type=jnp.float32)
    d_value = jnp.einsum(
        "hts,thd->sd", probs.astype(BF16), d_heads, preferred_element_type=jnp.float32
    )
    d_query, d_query_g = norm_back(
        query.reshape(count, -1, dim), query_g, rotate_back(d_query * scale, cosine, sine)
    )
    d_key, d_key_g = norm_back(
        key[:, None], key_g, rotate_back((d_key * scale)[:, None], cosine, sine)
    )
    return d_query.reshape(count, -1), d_key[:, 0], d_value, d_query_g[None], d_key_g[None]


def paired_plan(
    tokens,
    layer_inputs,
    cotangent,
    doc_lengths,
    w_query,
    w_key,
    w_value,
    w_output,
    laurel_left,
    laurel_right,
    w_gate,
    w_up,
    w_down,
    w_plgate,
    w_plproj,
    g_input,
    g_query,
    g_key,
    g_attn,
    g_laurel,
    g_preffw,
    g_ffw,
    g_perlayer,
):
    f32 = jnp.float32
    batch_at = lax.axis_index("batch")
    y_at, x_at = batch_at // 2, batch_at % 2
    core = lax.axis_index("seq")
    depth = lax.axis_size("fsdp")
    shards = lax.axis_size("batch") * lax.axis_size("seq") * depth
    shard_at = (batch_at * 2 + core) * depth + lax.axis_index("fsdp")
    rows = w_query.shape[0]
    model = rows * shards
    half_model, quarter_model = model // 2, model // 4
    tok_rows = tokens.shape[1]
    seq_rows = 2 * tok_rows
    head_dim = g_query.shape[0] * shards
    head_part = g_query.shape[0]
    score_scale = head_dim ** (-0.5)
    rank, pl_width = laurel_left.shape[1], w_plgate.shape[1]
    ff_width = w_gate.shape[1]
    ff_part = ff_width // 4
    query_width, kv_width = w_query.shape[1] // 2, w_key.shape[1] // 2
    small_used = 2 * rank + 2 * pl_width
    small_width = -(-small_used // 256) * 256

    own_gains = jnp.stack([g_input, g_attn, g_laurel, g_preffw, g_ffw, g_perlayer]).astype(f32)
    head_gains = jnp.stack([g_query, g_key]).astype(f32)
    table = jnp.zeros((8, model), f32)
    table = lax.dynamic_update_slice(table, own_gains, (0, shard_at * rows))
    table = lax.dynamic_update_slice(table, head_gains, (6, shard_at * head_part))
    gain_table = sum_all(table)
    query_g, key_g = gain_table[6:7, :head_dim], gain_table[7:8, :head_dim]
    model_g = halves_by(y_at, gain_table[:6], 1)
    input_g, attn_g, laurel_g, preffw_g, ffw_g, perlayer_g = [model_g[i] for i in range(6)]

    def core_half(array):
        pair = array.reshape(rows, 2, -1)
        return pick(pair, 1, core), pick(pair, 1, 1 - core)

    def ff_block(array):
        parts = array.reshape(rows, 2, 2, ff_part)
        keep, send = pick(parts, 2, core), pick(parts, 2, 1 - core)
        both = in_order(core, keep, swap_core(send), 0)
        return pick(both, 2, x_at), pick(both, 2, 1 - x_at)

    def ff_exchange(keep, send):
        return in_order(x_at, keep, swap_x(send), 0).reshape(4, rows, ff_part)

    small_own = jnp.concatenate(
        [
            laurel_left,
            laurel_right,
            w_plgate,
            w_plproj,
            jnp.zeros((rows, small_width - small_used), BF16),
        ],
        1,
    )
    first_keep, first_send = zip(
        *[core_half(entry) for entry in (w_query, w_key, w_value, small_own)]
    )
    first_keep = jnp.concatenate(first_keep, 1)
    first_block = in_order(core, first_keep, swap_core(jnp.concatenate(first_send, 1)), 0)
    first_z = jnp.concatenate(gather_z(first_block), 0)
    out_keep, out_send = core_half(w_output)
    gate_four = ff_exchange(*ff_block(w_gate))
    up_keep, up_send = ff_block(w_up)
    up_four = ff_exchange(up_keep, after(up_send, gate_four))
    down_keep, down_send = ff_block(w_down)
    down_four = ff_exchange(down_keep, after(down_send, up_four))
    out_block = in_order(core, out_keep, swap_core(out_send), 0)
    gate_z = gather_z(after(gate_four, first_block))
    out_z = jnp.concatenate(gather_z(after(out_block, gate_four)), 0)
    up_z = gather_z(after(up_four, out_block))
    ff_half = ff_part // 2
    down_later = after(down_four[:, :, ff_half:], up_four)
    down_z = gather_z(down_later)
    down_early = down_four[:, :, :ff_half]
    down_both = jnp.concatenate([down_early, swap_y(down_early)], 0)
    down_eight = gather_z(after(down_both, down_later))

    resid_in = halves_by(y_at, tokens[0], 1).astype(f32)
    upstream = halves_by(y_at, cotangent[0], 1).astype(f32)
    perlayer = layer_inputs[0].astype(f32)
    own_places = core * tok_rows + jnp.arange(tok_rows, dtype=jnp.int32)
    other_places = (1 - core) * tok_rows + jnp.arange(tok_rows, dtype=jnp.int32)
    places = jnp.concatenate([own_places, other_places])
    segment, rel_pos = positions_of(places, doc_lengths[0])
    cosine, sine = rope_tables(rel_pos, head_dim)
    distance = places[:, None] - places[None, :]
    allowed = (
        (segment[:, None] == segment[None, :]) & (distance >= 0) & (distance < WINDOW)
    )

    def with_partner(own):
        return jnp.concatenate([own, swap_core(own)], 0)

    x_normed = rms_norm(resid_in, input_g)
    x_low = x_normed.astype(BF16)
    x_own_pairs = lax.optimization_barrier(to_pairs(x_at, x_low, 1))
    first_z = after(first_z, (down_both, gain_table))
    first_x, first_y = swap_x(first_z), swap_y(first_z)
    x_pairs, cosine, sine, upstream = lax.optimization_barrier(
        (with_partner(x_own_pairs), cosine, sine, upstream)
    )
    part = first_z.shape[0] // 2
    first_corner = [
        swap_y(after(first_x[:part], (x_pairs, cosine))),
        swap_x(after(first_y[part:], (x_pairs, cosine))),
    ]
    first_w = jnp.concatenate([first_z, first_y, first_x] + first_corner, 0)
    gate_far = chained(swap_y, gate_z, first_corner)

    query_raw = project(x_pairs, first_w[:, :query_width])
    key_raw = project(x_pairs, first_w[:, query_width : query_width + kv_width])
    value_low = project(
        x_pairs, first_w[:, query_width + kv_width : query_width + 2 * kv_width]
    ).astype(BF16)
    small_mine = first_w[:, query_width + 2 * kv_width :]
    small_mine = after(small_mine, query_raw)
    small_pair = in_order(core, small_mine, swap_core(small_mine), 0)
    small_all = from_pairs(x_at, jnp.concatenate([small_pair[0], small_pair[1]], 1), 0)
    left_w, right_w, plgate_w, plproj_w = split_columns(
        small_all, [rank, rank, pl_width, pl_width]
    )
    out_z = after(out_z, query_raw)
    query_raw = after(query_raw, gate_far[0])
    out_x, out_y = swap_x(out_z), swap_y(out_z)
    attn_heads, query_low, key_low, lse = attend(
        query_raw, key_raw, value_low, cosine, sine, query_g[0], key_g[0], allowed, score_scale
    )
    out_x, out_y, attn_heads = lax.optimization_barrier(
        (out_x, out_y, after(attn_heads, gate_far[1]))
    )
    attn_low = attn_heads.astype(BF16)
    out_corner = [swap_y(out_x[:part]), swap_x(out_y[part:])]
    output_w = jnp.concatenate([out_z, out_y, out_x] + out_corner, 0)
    up_far = chained(swap_y, up_z, gate_far)
    down_far = chained(swap_y, down_z, up_far)
    def side_by_side(early, late):
        whole = jnp.zeros((model, ff_part), BF16)
        whole = lax.dynamic_update_slice(whole, jnp.concatenate(early, 0), (0, 0))
        return lax.dynamic_update_slice(whole, jnp.concatenate(late, 0), (0, ff_half))

    left_low = project(x_low, left_w).astype(BF16)
    right_out = against_rows(left_low, right_w)
    attn_keep, attn_send = onto_model([attn_low], [output_w])
    attn_proj = from_pairs(x_at, attn_keep + swap_core(attn_send).astype(f32), 1)
    hidden = (
        resid_in + rms_norm(attn_proj, attn_g) + x_normed + rms_norm(right_out, laurel_g)
    ) * ROOT_HALF

    def sum_near_and_far(near_of, far):
        far_sum = (far[0] + swap_core(far[1]).astype(f32)).astype(BF16)
        crossed = swap_x(far_sum)
        near = near_of(far_sum)
        return near[0] + swap_core(near[1]).astype(f32), crossed, near

    ffw_in = rms_norm(hidden, preffw_g).astype(BF16)
    ffw_far = swap_x(ffw_in)
    ffw_near = with_partner(ffw_in)
    gate_w, up_w = [
        jnp.concatenate([after(mine[0], ffw_near)] + mine[1:] + far, 0)
        for mine, far in ((gate_z, gate_far), (up_z, up_far))
    ]
    gates_near, ups_near, act_near = gate_up_act(ffw_near, gate_w, up_w)
    ffw_far = with_partner(after(ffw_far, act_near))
    down_w = side_by_side([after(down_eight[0], act_near)] + down_eight[1:], down_z + down_far)
    gates_far, ups_far, act_far = gate_up_act(after(ffw_far, down_far[0]), gate_w, up_w)
    downs_far = onto_model([act_far], [down_w])
    down_terms, crossed, _ = sum_near_and_far(
        lambda earlier: onto_model([after(act_near, earlier)], [down_w]), downs_far
    )
    down_terms = down_terms + crossed.astype(f32)
    second = hidden + rms_norm(down_terms, ffw_g)
    second_low = second.astype(BF16)
    plgate_out = project(second_low, plgate_w)
    gated_low = geglu(plgate_out, perlayer).astype(BF16)
    plproj_out = against_rows(gated_low, plproj_w)
    mixed_out = halves_by(y_at, (second + rms_norm(plproj_out, perlayer_g)).astype(BF16), 1)

    d_plproj, d_perlayer_g = norm_back(plproj_out, perlayer_g, upstream)
    d_plproj_low = d_plproj.astype(BF16)
    d_gated = project(d_plproj_low, plproj_w)
    d_plgate_low = jax.vjp(geglu, plgate_out, perlayer)[1](d_gated)[0].astype(BF16)
    d_second = upstream + against_rows(d_plgate_low, plgate_w)
    d_down, d_ffw_g = norm_back(down_terms, ffw_g, d_second)
    d_down_low = d_down.astype(BF16)
    d_down_far = swap_x(d_down_low)
    d_down_near = with_partner(d_down_low)
    d_gate_near, d_up_near = gate_up_back(d_down_near, down_w, gates_near, ups_near)
    d_down_far = with_partner(after(d_down_far, d_gate_near))

    ff_split = (4, depth, rows)

    def ff_send(sides, first_column=0, width=ff_part):
        cut = [(left, [(right, first_column, width)]) for left, right in sides]
        return weight_sum(cut, half_model, half_model, ff_split)

    def ff_keep(sides, received, first_column=0, width=ff_part):
        cut = [(left, [(right, first_column, width)]) for left, right in sides]
        return weight_sum(cut, 0, half_model, ff_split, received, True)

    def ff_owned(four):
        four = four.reshape(2, 2, rows, ff_part)
        keep, send = pick(four, 0, x_at), pick(four, 0, 1 - x_at)
        over = swap_x(send)
        a, b = pick(keep, 0, core), pick(over, 0, core)
        crossed = swap_core(jnp.stack([pick(keep, 0, 1 - core), pick(over, 0, 1 - core)]))
        quarters = []
        for x_of in range(2):
            near = jnp.where(x_at == x_of, a, b)
            far = jnp.where(x_at == x_of, crossed[0], crossed[1])
            quarters += [
                jnp.where(core == c_of, near, far).astype(f32) for c_of in range(2)
            ]
        return jnp.concatenate(quarters, 1)

    down_sides = [(d_down_near, act_near), (d_down_far, act_far)]
    down_sent = ff_send(down_sides, ff_half, ff_half)
    down_near = chained(swap_y, down_sent)
    whole_cut = [(left, [(right, 0, ff_half)]) for left, right in down_sides]
    down_whole = weight_sum(whole_cut, 0, model, (8, depth, rows), (), True)
    down_eight = scatter_z(down_whole)
    d_gate_far, d_up_far = gate_up_back(
        d_down_far, down_w, after(gates_far, down_near[0]), ups_far
    )
    gate_sides = [(ffw_near, d_gate_near), (ffw_far, d_gate_far)]
    up_sides = [(ffw_near, d_up_near), (ffw_far, d_up_far)]
    ffw_weights = [gate_w, up_w]
    gate_sent = ff_send(gate_sides)
    gate_near = chained(swap_y, gate_sent, down_near)
    d_ffw_far = onto_model([d_gate_far, d_up_far], ffw_weights)
    d_ffw_terms, crossed, d_ffw_near = sum_near_and_far(
        lambda earlier: onto_model(
            [after(d_gate_near, (earlier, gate_near[0], down_eight)), d_up_near], ffw_weights
        ),
        d_ffw_far,
    )
    up_sent = ff_send(up_sides)
    up_near = chained(swap_y, up_sent, gate_near)
    down_near = [after(down_near[0], up_sent)] + down_near[1:]
    down_kept = ff_keep(down_sides, down_near, ff_half, ff_half)
    down_four = scatter_z(down_kept)
    gate_near = [after(gate_near[0], down_kept)] + gate_near[1:]
    gate_kept = ff_keep(gate_sides, gate_near)
    gate_four = scatter_z(gate_kept)
    d_ffw_terms = d_ffw_terms + after(crossed, gate_kept).astype(f32)

    d_hidden_norm, d_preffw_g = norm_back(hidden, preffw_g, d_ffw_terms)
    d_branch = (d_second + d_hidden_norm) * ROOT_HALF
    d_laurel, d_laurel_g = norm_back(right_out, laurel_g, d_branch)
    d_laurel_low = d_laurel.astype(BF16)
    d_left_low = project(d_laurel_low, right_w).astype(BF16)
    d_attn, d_attn_g = norm_back(attn_proj, attn_g, d_branch)
    d_attn_pairs = with_partner(lax.optimization_barrier(to_pairs(x_at, d_attn.astype(BF16), 1)))

    pair_split = (2, depth, rows)

    def whole_columns(keep, received):
        ends = [jnp.where(core == c_of, keep, received).astype(f32) for c_of in range(2)]
        return jnp.concatenate(ends, 1)

    def pair_owned(pair):
        pair = pair.reshape(2, rows, pair.shape[1])
        keep, send = pick(pair, 0, core), pick(pair, 0, 1 - core)
        return keep, swap_core(send)

    def pair_send(sides):
        return weight_sum(sides, half_model, half_model, pair_split)

    def pair_pass(sides, over_x):
        return weight_sum(sides, quarter_model, quarter_model, pair_split, over_x[2:])

    def pair_keep(sides, over_x, over_y):
        got = list(zip(over_x[:2], over_y))
        return weight_sum(sides, 0, quarter_model, pair_split, got, True)

    out_sides = [(d_attn_pairs, [(attn_low, 0, query_width)])]
    out_sent = pair_send(out_sides)
    out_near = chained(swap_x, out_sent[2:] + out_sent[:2])
    out_near = out_near[2:] + out_near[:2]
    d_heads = project(d_attn_pairs, output_w)
    d_heads = after(d_heads, (up_near[1], down_four, out_near[2:]))
    d_query_low, d_key_low, d_value_low, d_query_g, d_key_g = attend_back(
        d_heads,
        query_raw,
        key_raw,
        query_low,
        key_low,
        value_low,
        lse,
        cosine,
        sine,
        query_g[0],
        key_g[0],
        allowed,
        score_scale,
    )

    up_kept = ff_keep(up_sides, [after(up_near[0], d_heads)] + up_near[1:])
    up_four = scatter_z(up_kept)
    d_query_low = after(d_query_low, (out_near[:2], up_kept))
    d_query_low, d_key_low, d_value_low = [
        entry.astype(BF16) for entry in (d_query_low, d_key_low, d_value_low)
    ]
    first_rights = [
        (d_query_low, 0, query_width),
        (d_key_low, 0, kv_width),
        (d_value_low, 0, kv_width),
    ]
    first_sides = [(x_pairs, first_rights)]
    first_sent = pair_send(first_sides)
    first_near = chained(swap_x, first_sent[2:] + first_sent[:2], out_near[:2])
    first_near = first_near[2:] + first_near[:2]
    small_halves = small_sums(
        [x_low, d_laurel_low, second_low, d_plproj_low],
        [d_left_low, left_low, d_plgate_low, gated_low],
        small_width,
    )
    small_sum = pick(small_halves, 1, core).astype(f32) + swap_core(
        pick(small_halves, 1, 1 - core)
    ).astype(f32)
    small_sum = small_sum.astype(BF16).reshape(2, 2, quarter_model, small_width // 2)
    over_x = swap_x(pick(small_sum, 1, 1 - x_at))
    small_sum = pick(small_sum, 1, x_at).astype(f32) + over_x.astype(f32)
    small_sum = small_sum[0] + swap_y(small_sum[1].astype(BF16)).astype(f32)
    small_sum = small_sum.reshape(2, depth, rows, small_width // 2).astype(BF16)
    small_pair = scatter_z_small(jnp.transpose(small_sum, (1, 0, 2, 3)))
    small_keep, small_send = pick(small_pair, 0, core), pick(small_pair, 0, 1 - core)
    out_right = out_sides[0][1]
    out_near = out_near[:2] + [after(out_near[2], up_kept), out_near[3]]
    out_passed = pair_pass([(d_attn_pairs, out_right)], out_near)
    out_over = chained(swap_y, out_passed, up_near)
    first_w_parts = split_columns(
        first_w[:, : query_width + 2 * kv_width], [query_width, kv_width, kv_width]
    )
    d_x_keep, d_x_send = onto_model([d_query_low, d_key_low, d_value_low], first_w_parts)
    d_x_terms = from_pairs(x_at, d_x_keep + swap_core(d_x_send).astype(f32), 1)
    d_x_terms = d_x_terms + against_rows(d_left_low, left_w)
    d_input, d_input_g = norm_back(resid_in, input_g, d_x_terms + d_branch)
    grad_tokens = halves_by(y_at, d_input + d_branch, 1)[None]

    widths = [query_width, kv_width, kv_width]
    first_passed = pair_pass([(x_pairs, first_rights)], first_near)
    first_over = chained(swap_y, first_passed, out_over)
    out_over = [after(out_over[0], up_four)] + out_over[1:]
    out_kept = pair_keep([(d_attn_pairs, out_right)], out_near, out_over)
    out_four = scatter_z(out_kept)
    first_kept = pair_keep([(x_pairs, first_rights)], first_near, first_over)
    first_four = scatter_z(first_kept)
    grad_output = whole_columns(*pair_owned(out_four))
    first_keep, first_received = pair_owned(first_four)
    grad_query, grad_key, grad_value = [
        whole_columns(keep, received)
        for keep, received in zip(
            split_columns(first_keep, widths), split_columns(first_received, widths)
        )
    ]

    grad_left, grad_right, grad_plgate, grad_plproj = split_columns(
        whole_columns(small_keep, swap_core(small_send)), [rank, rank, pl_width, pl_width]
    )

    down_eight, down_four = after((down_eight, down_four), first_near)
    down_eight = down_eight.reshape(2, 4, rows, ff_half)
    down_last = down_eight[0].astype(f32) + swap_y(down_eight[1]).astype(f32)
    grad_down = ff_owned(
        jnp.concatenate([down_last.astype(BF16), down_four.reshape(4, rows, ff_half)], 2)
    )
    grad_gate = ff_owned(after(gate_four, first_near))
    grad_up = ff_owned(after(up_four, first_near))

    gain_grads = jnp.stack(
        [d_input_g, d_attn_g, d_laurel_g, d_preffw_g, d_ffw_g, d_perlayer_g]
    )
    head_grads = jnp.pad(
        jnp.concatenate([d_query_g, d_key_g], 0), ((0, 0), (0, model - head_dim))
    )
    gain_sums = sum_all(jnp.concatenate([halves_by(y_at, gain_grads, 1), head_grads], 0))
    own_sums = lax.dynamic_slice(gain_sums, (0, shard_at * rows), (6, rows))
    own_heads = lax.dynamic_slice(gain_sums, (6, shard_at * head_part), (2, head_part))
    (
        grad_g_input,
        grad_g_attn,
        grad_g_laurel,
        grad_g_preffw,
        grad_g_ffw,
        grad_g_perlayer,
    ) = [own_sums[i] for i in range(6)]
    grad_g_query, grad_g_key = own_heads[0], own_heads[1]
    return (
        mixed_out[None],
        grad_tokens,
        grad_query,
        grad_key,
        grad_value,
        grad_output,
        grad_left,
        grad_right,
        grad_gate,
        grad_up,
        grad_down,
        grad_plgate,
        grad_plproj,
        grad_g_input,
        grad_g_query,
        grad_g_key,
        grad_g_attn,
        grad_g_laurel,
        grad_g_preffw,
        grad_g_ffw,
        grad_g_perlayer,
    )


def solution(mesh):
    paired = mesh.shape["batch"] == 4 and mesh.shape["seq"] == 2
    by_token = P(ROW_AXES, "seq", None)
    by_row = P(ALL_AXES, None)
    by_entry = P(ALL_AXES)
    return jax.shard_map(
        paired_plan if paired else whole_gather_plan,
        mesh=mesh,
        in_specs=(by_token,) * 3 + (P(ROW_AXES, None),) + (by_row,) * 11 + (by_entry,) * 8,
        out_specs=(by_token,) * 2 + (by_row,) * 11 + (by_entry,) * 8,
        check_vma=False,
    )
```
